128 devices in a mesh: ctx: 32 (over z, y, core), head: 4 (over x).
Axes of the slice: x: 4, y: 4, z: 4, core: 2. Of those that a mesh axis runs over, the one named last changes fastest.
Arguments:
- queries: bfloat16 [32768, 3072], P(('ctx', 'head')), may hold values from -6 to 6
- keys: bfloat16 [32768, 3072], P(('ctx', 'head')), may hold values from -6 to 6
- values: bfloat16 [32768, 3072], P(('ctx', 'head')), may hold values from -6 to 6
- outputs: bfloat16 [32768, 3072], P(('ctx', 'head')), may hold values from -6 to 6
- out_grad: bfloat16 [32768, 3072], P(('ctx', 'head')), may hold values from -4 to 4
- logsumexp: float32 [24, 32768], P('head', 'ctx'), may hold values from 2.5 to 4.5
- clip_of_group: int32 [32], replicated, may hold values from 0 to 15, never falling along the last dimension, each value on 1 to 3 neighbouring positions
Outputs:
- query_grad: bfloat16 [32768, 3072], P(('ctx', 'head'))
- key_grad: bfloat16 [32768, 3072], P(('ctx', 'head'))
- value_grad: bfloat16 [32768, 3072], P(('ctx', 'head'))
The draws below stay inside these ranges and needn't reach their ends.
Inputs may be any that keep to these rules, and one draw needn't show every extreme that they name: `clip_of_group`: never falls along the groups; each clip holds 1 to 3 consecutive groups, and some clip holds exactly 3.
All inputs are finite; a program needn't handle non-finite values.
Results may differ from the reference program's by a relative error of at most 0.006.
Values may be sent and summed in bfloat16 or wider, within the bound.
A program may use at most 256 MiB of HBM per device.

```python
import math
import jax
import jax.numpy as jnp
import numpy as np
from jax import lax

H = 24
HD = 128
GROUP = 1024
MOST = 3
NGROUP = 32
CLIPS = 16
TOKENS = 32768


def block_levels(rng, shape, cuts, smallest, high):
    loudness, own = 1.0, jax.random.fold_in(rng, 6)
    for position, parts in cuts:
        steps = jnp.exp(jax.random.uniform(jax.random.fold_in(own, position), (parts,), jnp.float32, smallest / len(cuts), high / len(cuts)))
        loudness = loudness * jnp.repeat(steps, shape[position] // parts).reshape([-1 if axis == position else 1 for axis in range(len(shape))])
    return loudness


def split_up(amount, total, limit, slope):
    loads = [(1 << 20) // math.isqrt(grade ** slope) + 1 for grade in range(2, amount + 1)]
    rest, given = total - limit - (amount - 1), [1] * (amount - 1)
    while rest > 0:
        movable = [i for i in range(amount - 1) if given[i] < limit]
        pool, budget = sum([loads[i] for i in movable]), rest
        for i in movable:
            more = min(limit - given[i], max(1, budget * loads[i] // pool), rest)
            given[i] = given[i] + more
            rest = rest - more
    return np.array([limit] + given)


def ragged(stream_key, number_of, total, most, skew):
    if number_of == 2:
        one = jax.random.randint(stream_key, (), max(1, total - most), min(most, total - 1) + 1)
        return jnp.stack([one, total - one])
    sizes = jnp.asarray(split_up(number_of, total, most, skew), jnp.int32)
    pairs = (number_of - 1) // 2
    giver, taker = sizes[1:1 + 2 * pairs:2], sizes[2:2 + 2 * pairs:2]
    slack = jnp.minimum(giver - 1, most - taker)
    passed = jax.random.randint(jax.random.fold_in(stream_key, 1), (pairs,), 0, 1 << 20) % (slack + 1)
    sizes = sizes.at[1:1 + 2 * pairs:2].set(giver - passed).at[2:2 + 2 * pairs:2].set(taker + passed)
    return sizes[jax.random.permutation(jax.random.fold_in(stream_key, 2), number_of)]


def scatter_about(stream_key, extent, spread, reach, cuts=(), held_as=jnp.bfloat16):
    values = spread * jax.random.normal(stream_key, extent, jnp.float32)
    if cuts:
        values = values * block_levels(stream_key, extent, cuts, -0.22, 0.18)
    return jnp.clip(values, -reach, reach).astype(held_as)


def setup_inputs(seed: int = 0) -> dict:
    key_list = jax.random.split(jax.random.key(seed), 8)
    return {
        "queries": scatter_about(key_list[0], (TOKENS, H * HD), 1.0, 6.0, ((0, 128),)),
        "keys": scatter_about(key_list[1], (TOKENS, H * HD), 1.0, 6.0, ((0, 128),)),
        "values": scatter_about(key_list[2], (TOKENS, H * HD), 1.0, 6.0, ((0, 128),)),
        "outputs": scatter_about(key_list[3], (TOKENS, H * HD), 1.0, 6.0, ((0, 128),)),
        "out_grad": scatter_about(key_list[4], (TOKENS, H * HD), 0.3, 4.0, ((0, 128),)),
        "logsumexp": jnp.clip(2.5 + 2.0 * jax.random.uniform(key_list[5], (H, TOKENS), jnp.float32) ** block_levels(key_list[5], (H, TOKENS), ((0, 4), (1, 32)), -0.2, 0.2), 2.5, 4.5),
        "clip_of_group": jnp.searchsorted(jnp.cumsum(ragged(key_list[6], CLIPS, NGROUP, MOST, 2)), jnp.arange(NGROUP), side="right").astype(jnp.int32),
    }


def tile_grads(query_block, key_block, value_block, grad_block, lse_block, delta_block, visible):
    scale = query_block.shape[-1] ** -0.5
    query_f = query_block.astype(jnp.float32)
    key_f = key_block.astype(jnp.float32)
    value_f = value_block.astype(jnp.float32)
    grad_f = grad_block.astype(jnp.float32)
    scores = jnp.einsum("qhd,khd->hqk", query_f, key_f) * scale
    prob = jnp.where(visible[None], jnp.exp(scores - lse_block[:, :, None]), 0.0)
    prob_b = lax.optimization_barrier(prob.astype(jnp.bfloat16)).astype(jnp.float32)
    value_part = jnp.einsum("hqk,qhd->khd", prob_b, grad_f)
    dprob = jnp.einsum("qhd,khd->hqk", grad_f, value_f)
    dscore = prob * (dprob - delta_block[:, :, None])
    dscore = lax.optimization_barrier(dscore.astype(jnp.bfloat16)).astype(jnp.float32)
    query_part = jnp.einsum("hqk,khd->qhd", dscore, key_f) * scale
    key_part = jnp.einsum("hqk,qhd->khd", dscore, query_f) * scale
    return query_part, key_part, value_part


def reference(queries, keys, values, outputs, out_grad, logsumexp, clip_of_group):
    heads = logsumexp.shape[0]
    width = queries.shape[1] // heads

    def split(array):
        return array.reshape(NGROUP, GROUP, heads, width)

    query_all = split(queries)
    key_all = split(keys)
    value_all = split(values)
    grad_all = split(out_grad)
    delta = jnp.sum(grad_all.astype(jnp.float32) * split(outputs).astype(jnp.float32), axis=-1)
    delta_all = jnp.transpose(delta, (0, 2, 1))
    lse_all = jnp.transpose(logsumexp.reshape(heads, NGROUP, GROUP), (1, 0, 2))
    front = MOST - 1
    key_pad = jnp.concatenate([jnp.zeros((front, GROUP, heads, width), jnp.bfloat16), key_all], axis=0)
    value_pad = jnp.concatenate([jnp.zeros((front, GROUP, heads, width), jnp.bfloat16), value_all], axis=0)
    clip_pad = jnp.concatenate([-jnp.ones((front,), jnp.int32), clip_of_group.astype(jnp.int32)], axis=0)

    def step(carry, index):
        key_acc, value_acc = carry
        key_win = lax.dynamic_slice_in_dim(key_pad, index, MOST, 0).reshape(MOST * GROUP, heads, width)
        value_win = lax.dynamic_slice_in_dim(value_pad, index, MOST, 0).reshape(MOST * GROUP, heads, width)
        clip_win = lax.dynamic_slice_in_dim(clip_pad, index, MOST, 0)
        own_clip = lax.dynamic_index_in_dim(clip_of_group.astype(jnp.int32), index, 0, keepdims=False)
        same = jnp.repeat(clip_win == own_clip, GROUP)
        visible = jnp.broadcast_to(same[None, :], (GROUP, MOST * GROUP))
        query_part, key_part, value_part = tile_grads(
            query_all[index], key_win, value_win, grad_all[index], lse_all[index], delta_all[index], visible)
        key_old = lax.dynamic_slice_in_dim(key_acc, index, MOST, 0)
        value_old = lax.dynamic_slice_in_dim(value_acc, index, MOST, 0)
        key_acc = lax.dynamic_update_slice_in_dim(key_acc, key_old + key_part.reshape(MOST, GROUP, heads, width), index, 0)
        value_acc = lax.dynamic_update_slice_in_dim(value_acc, value_old + value_part.reshape(MOST, GROUP, heads, width), index, 0)
        return (key_acc, value_acc), query_part

    start = jnp.zeros((NGROUP + front, GROUP, heads, width), jnp.float32)
    (key_acc, value_acc), query_parts = lax.scan(step, (start, start), jnp.arange(NGROUP, dtype=jnp.int32))
    total = NGROUP * GROUP
    query_grad = query_parts.reshape(total, heads * width).astype(jnp.bfloat16)
    key_grad = key_acc[front:].reshape(total, heads * width).astype(jnp.bfloat16)
    value_grad = value_acc[front:].reshape(total, heads * width).astype(jnp.bfloat16)
    return query_grad, key_grad, value_grad
```

```python
import functools

import jax
import jax.numpy as jnp
from jax import lax
from jax.experimental import pallas as pl
from jax.experimental.pallas import tpu as pltpu
from jax.sharding import PartitionSpec as P

HD = 128
GROUP = 1024
HEADS = 6
RANKS = 4
COUNT = 32
ROWS = GROUP // RANKS
BQ = 256
MESH = pl.DeviceIdType.MESH
SCALE = HD**-0.5
LOG2E = 1.4426950408889634
HIDDEN = 1e30
f32, bf16 = jnp.float32, jnp.bfloat16


def dot(a, b, ca, cb):
    return lax.dot_general(a, b, (((ca,), (cb,)), ((), ())), preferred_element_type=f32)


def kernel(
    q_in, k_in, v_in, o_in, g_in, lse_in, clip_in,
    q_out, k_out, v_out,
    qg, kv, own, dq, part, relay, back1, back2, stage, o_loc, g_loc, dl_src, dl, lse3,
    in_send, in_recv, kv_send, kv_recv, part_send, relay_recv, back_recv,
    out_send, out_recv, dl_send, dl_recv, loc,
):
    x = lax.axis_index("head")
    c = lax.axis_index("ctx")
    even = lax.rem(c, 2) == 0
    odd = lax.rem(c, 2) == 1

    def rank(p):
        return lax.rem(x + p, RANKS)

    def at_rank(p):
        return {"head": rank(p)}

    def at_ctx(d):
        return {"ctx": lax.rem(c + d + COUNT, COUNT)}

    def arrived(ref, sem):
        pltpu.make_async_copy(ref, ref, sem).wait()

    def remote(src, dst, send, recv, device):
        pltpu.make_async_remote_copy(
            src_ref=src, dst_ref=dst, send_sem=send, recv_sem=recv,
            device_id=device, device_id_type=MESH,
        ).start()

    get_o = pltpu.make_async_copy(o_in, o_loc, loc.at[0])
    get_g = pltpu.make_async_copy(g_in, g_loc, loc.at[1])
    get_o.start()
    get_g.start()

    barrier = pltpu.get_barrier_semaphore()
    for p in range(1, RANKS):
        pl.semaphore_signal(barrier, inc=1, device_id=at_rank(p), device_id_type=MESH)
    for d in (-2, -1, 1, 2):
        pl.semaphore_signal(barrier, inc=1, device_id=at_ctx(d), device_id_type=MESH)
    pl.semaphore_wait(barrier, RANKS - 1 + 4)

    mine = pl.ds(pl.multiple_of(x * ROWS, ROWS), ROWS)

    def fetch(kind, h):
        pair = ((k_in, kv.at[0, h, 0]), (v_in, kv.at[0, h, 1]))
        if kind == 1:
            pair = ((q_in, qg.at[h, 0]), (g_in, qg.at[h, 1]))
        for src, dst in pair:
            for p in (1, 3, 2, 0):
                cols = pl.ds(pl.multiple_of((rank(p) * HEADS + h) * HD, HD), HD)
                if p == 0:
                    pltpu.make_async_copy(src.at[:, cols], dst.at[mine], in_recv.at[kind, h]).start()
                else:
                    remote(src.at[:, cols], dst.at[mine], in_send.at[kind, h], in_recv.at[kind, h], at_rank(p))

    def fetch_head(h, _):
        fetch(0, h)
        fetch(1, h)
        return 0

    lax.fori_loop(0, HEADS, fetch_head, 0)

    get_o.wait()
    get_g.wait()
    lane = lax.broadcasted_iota(jnp.int32, (ROWS, HD), 1)
    delta = jnp.zeros((ROWS, HD), f32)
    for r in range(RANKS):
        for h in range(HEADS):
            cols = pl.ds((r * HEADS + h) * HD, HD)
            prod = o_loc[:, cols].astype(f32) * g_loc[:, cols].astype(f32)
            total = jnp.sum(prod, axis=1, keepdims=True)
            delta = jnp.where(lane == r * 8 + h, total, delta)
    flipped = delta.T
    for r in range(RANKS):
        dl_src[r] = flipped[r * 8 : (r + 1) * 8]
    for p in range(RANKS):
        if p == 0:
            pltpu.make_async_copy(dl_src.at[x], dl.at[:, mine], dl_recv).start()
        else:
            remote(dl_src.at[rank(p)], dl.at[:, mine], dl_send, dl_recv, at_rank(p))

    here = clip_in[c]
    lse = lse_in[...] * LOG2E
    lse3[0] = lse
    for j in (1, 2):
        seen = jnp.logical_and(clip_in[lax.max(c - j, 0)] == here, c >= j)
        lse3[j] = jnp.where(seen, lse, HIDDEN)
    arrived(dl, dl_recv)

    def give(h):
        arrived(kv.at[0, h], in_recv.at[0, h])
        remote(kv.at[0, h], kv.at[1, h], kv_send.at[0, h], kv_recv.at[0, h], at_ctx(1))

        @pl.when(even)
        def _():
            remote(kv.at[0, h], kv.at[2, h], kv_send.at[1, h], kv_recv.at[1, h], at_ctx(2))

    def grads(h, j):
        key = kv[j, h, 0]
        value = kv[j, h, 1]
        dk = jnp.zeros((GROUP, HD), f32)
        dv = jnp.zeros((GROUP, HD), f32)
        for t in range(GROUP // BQ):
            rows = pl.ds(t * BQ, BQ)
            query = qg[h, 0, rows]
            grad = qg[h, 1, rows]
            score = dot(key, query, 1, 1)
            prob = jnp.exp2(score * (SCALE * LOG2E) - lse3[j, pl.ds(h, 1), rows])
            dprob = dot(value, grad, 1, 1)
            dscore = (prob * (dprob - dl[pl.ds(h, 1), rows])).astype(bf16)
            dv += dot(prob.astype(bf16), grad, 1, 0)
            dk += dot(dscore, query, 1, 0)
            step = dot(dscore, key, 0, 0)
            if j == 0:
                dq[h, rows] = step
            elif j == 1:
                dq[h, rows] += step
            else:
                stage[0, h, rows] = ((dq[h, rows] + step) * SCALE).astype(bf16)
        if j == 0:
            own[h, 0] = dk
            own[h, 1] = dv
        else:
            part[j - 1, h, 0] = dk.astype(bf16)
            part[j - 1, h, 1] = dv.astype(bf16)

    def put(which, out, h):
        cols = pl.ds(pl.multiple_of((x * HEADS + h) * HD, HD), HD)
        for p in (1, 3, 2, 0):
            src = stage.at[which, h, pl.ds(pl.multiple_of(rank(p) * ROWS, ROWS), ROWS)]
            if p == 0:
                pltpu.make_async_copy(src, out.at[:, cols], out_recv.at[which]).start()
            else:
                remote(src, out.at[:, cols], out_send.at[which, h], out_recv.at[which], at_rank(p))

    give(0)

    def step(i, _):
        @pl.when(i < HEADS)
        def _():
            arrived(qg.at[i], in_recv.at[1, i])
            grads(i, 0)

        @pl.when(i + 1 < HEADS)
        def _():
            give(i + 1)

        inner = jnp.logical_and(i >= 1, i <= HEADS)

        @pl.when(inner)
        def _():
            h = i - 1
            arrived(kv.at[1, h], kv_recv.at[0, h])

            @pl.when(even)
            def _():
                remote(kv.at[1, h], kv.at[2, h], kv_send.at[2, h], kv_recv.at[1, h], at_ctx(1))

            grads(h, 1)

            @pl.when(odd)
            def _():
                remote(part.at[0, h], back1.at[h], part_send.at[0, h], back_recv.at[0, h], at_ctx(-1))

            arrived(kv.at[2, h], kv_recv.at[1, h])
            grads(h, 2)

            @pl.when(odd)
            def _():
                remote(part.at[1, h], relay.at[h], part_send.at[1, h], relay_recv.at[h], at_ctx(-1))

            @pl.when(even)
            def _():
                remote(part.at[1, h], back2.at[h], part_send.at[1, h], back_recv.at[1, h], at_ctx(-2))

            put(0, q_out, h)

        @pl.when(i >= 2)
        def _():
            h = i - 2
            arrived(back1.at[h], back_recv.at[0, h])

            @pl.when(even)
            def _():
                arrived(back2.at[h], back_recv.at[1, h])
                dk = own[h, 0] + back1[h, 0].astype(f32) + back2[h, 0].astype(f32)
                dv = own[h, 1] + back1[h, 1].astype(f32) + back2[h, 1].astype(f32)
                stage[1, h] = (dk * SCALE).astype(bf16)
                stage[2, h] = dv.astype(bf16)

            @pl.when(odd)
            def _():
                stage[1, h] = ((own[h, 0] + back1[h, 0].astype(f32)) * SCALE).astype(bf16)
                stage[2, h] = (own[h, 1] + back1[h, 1].astype(f32)).astype(bf16)

            put(1, k_out, h)
            put(2, v_out, h)

        @pl.when(jnp.logical_and(inner, even))
        def _():
            h = i - 1
            arrived(relay.at[h], relay_recv.at[h])
            for n in range(2):
                part[0, h, n] = (part[0, h, n].astype(f32) + relay[h, n].astype(f32)).astype(bf16)
            remote(part.at[0, h], back1.at[h], part_send.at[0, h], back_recv.at[0, h], at_ctx(-1))

        return 0

    lax.fori_loop(0, HEADS + 2, step, 0)

    most = pl.ds(0, GROUP - ROWS)
    for r in range(1, RANKS):
        arrived(dl_src.at[r], dl_send)

    def drain(h, _):
        arrived(kv.at[0, h, :, most], in_send.at[0, h])
        arrived(qg.at[h, :, most], in_send.at[1, h])
        arrived(kv.at[0, h], kv_send.at[0, h])
        arrived(part.at[0, h], part_send.at[0, h])
        arrived(part.at[1, h], part_send.at[1, h])
        for n in range(3):
            arrived(stage.at[n, h, most], out_send.at[n, h])

        @pl.when(even)
        def _():
            arrived(kv.at[0, h], kv_send.at[1, h])
            arrived(kv.at[1, h], kv_send.at[2, h])

        return 0

    lax.fori_loop(0, HEADS, drain, 0)
    arrived(q_out, out_recv.at[0])
    arrived(k_out, out_recv.at[1])
    arrived(v_out, out_recv.at[2])


def local(queries, keys, values, outputs, out_grad, logsumexp, clip_of_group):
    hbm = pl.BlockSpec(memory_space=pl.ANY)
    vmem = pl.BlockSpec(memory_space=pltpu.VMEM)
    smem = pl.BlockSpec(memory_space=pltpu.SMEM)
    dma = pltpu.SemaphoreType.DMA
    whole = (2, GROUP, HD)
    out = jax.ShapeDtypeStruct((ROWS, RANKS * HEADS * HD), bf16)
    return pl.pallas_call(
        kernel,
        out_shape=(out, out, out),
        in_specs=[hbm, hbm, hbm, hbm, hbm, vmem, smem],
        out_specs=(hbm, hbm, hbm),
        scratch_shapes=[
            pltpu.VMEM((HEADS, *whole), bf16),
            pltpu.VMEM((3, HEADS, *whole), bf16),
            pltpu.VMEM((HEADS, *whole), f32),
            pltpu.VMEM((HEADS, GROUP, HD), f32),
            pltpu.VMEM((2, HEADS, *whole), bf16),
            pltpu.VMEM((HEADS, *whole), bf16),
            pltpu.VMEM((HEADS, *whole), bf16),
            pltpu.VMEM((HEADS, *whole), bf16),
            pltpu.VMEM((3, HEADS, GROUP, HD), bf16),
            pltpu.VMEM((ROWS, RANKS * HEADS * HD), bf16),
            pltpu.VMEM((ROWS, RANKS * HEADS * HD), bf16),
            pltpu.VMEM((RANKS, 8, ROWS), f32),
            pltpu.VMEM((8, GROUP), f32),
            pltpu.VMEM((3, HEADS, GROUP), f32),
            dma((2, HEADS)),
            dma((2, HEADS)),
            dma((3, HEADS)),
            dma((2, HEADS)),
            dma((2, HEADS)),
            dma((HEADS,)),
            dma((2, HEADS)),
            dma((3, HEADS)),
            dma((3,)),
            dma,
            dma,
            dma((2,)),
        ],
        cost_estimate=pl.CostEstimate(
            flops=2 * 5 * 3 * HEADS * GROUP * GROUP * HD,
            bytes_accessed=12 * 2**20,
            transcendentals=3 * HEADS * GROUP * GROUP,
        ),
        compiler_params=pltpu.CompilerParams(
            collective_id=0, has_side_effects=True, vmem_limit_bytes=58 * 2**20
        ),
        name="clip_attention_backward",
    )(queries, keys, values, outputs, out_grad, logsumexp, clip_of_group)


def solution(mesh):
    rows = P(("ctx", "head"), None)
    return jax.shard_map(
        local,
        mesh=mesh,
        in_specs=(rows, rows, rows, rows, rows, P("head", "ctx"), P()),
        out_specs=(rows, rows, rows),
        check_vma=False,
    )
```

```python
import functools

import jax
import jax.numpy as jnp
from jax import lax
from jax.experimental import pallas as pl
from jax.experimental.pallas import tpu as pltpu
from jax.sharding import PartitionSpec as P

HD = 128
GROUP = 1024
HEADS = 6
RANKS = 4
COUNT = 32
ROWS = GROUP // RANKS
BQ = 256
MESH = pl.DeviceIdType.MESH
SCALE = HD**-0.5
LOG2E = 1.4426950408889634
HIDDEN = 1e30
f32, bf16 = jnp.float32, jnp.bfloat16


def dot(a, b, ca, cb):
    return lax.dot_general(a, b, (((ca,), (cb,)), ((), ())), preferred_element_type=f32)


def kernel(
    q_in, k_in, v_in, o_in, g_in, lse_in, clip_in,
    q_out, k_out, v_out,
    qg, kv, own, dq, part, relay, back1, back2, stage, o_loc, g_loc, dl_src, dl, lse3,
    in_send, in_recv, kv_send, kv_recv, part_send, relay_recv, back_recv,
    out_send, out_recv, dl_send, dl_recv, loc,
):
    x = lax.axis_index("head")
    c = lax.axis_index("ctx")
    even = lax.rem(c, 2) == 0
    odd = lax.rem(c, 2) == 1

    def rank(p):
        return lax.rem(x + p, RANKS)

    def at_rank(p):
        return {"head": rank(p)}

    def at_ctx(d):
        return {"ctx": lax.rem(c + d + COUNT, COUNT)}

    def arrived(ref, sem):
        pltpu.make_async_copy(ref, ref, sem).wait()

    def remote(src, dst, send, recv, device):
        pltpu.make_async_remote_copy(
            src_ref=src, dst_ref=dst, send_sem=send, recv_sem=recv,
            device_id=device, device_id_type=MESH,
        ).start()

    get_o = pltpu.make_async_copy(o_in, o_loc, loc.at[0])
    get_g = pltpu.make_async_copy(g_in, g_loc, loc.at[1])
    get_o.start()
    get_g.start()

    barrier = pltpu.get_barrier_semaphore()
    for p in range(1, RANKS):
        pl.semaphore_signal(barrier, inc=1, device_id=at_rank(p), device_id_type=MESH)
    for d in (-2, -1, 1, 2):
        pl.semaphore_signal(barrier, inc=1, device_id=at_ctx(d), device_id_type=MESH)
    pl.semaphore_wait(barrier, RANKS - 1 + 4)

    mine = pl.ds(pl.multiple_of(x * ROWS, ROWS), ROWS)

    def fetch(kind, h):
        pair = ((k_in, kv.at[0, h, 0]), (v_in, kv.at[0, h, 1]))
        if kind == 1:
            pair = ((q_in, qg.at[h, 0]), (g_in, qg.at[h, 1]))
        for src, dst in pair:
            for p in (1, 3, 2, 0):
                cols = pl.ds(pl.multiple_of((rank(p) * HEADS + h) * HD, HD), HD)
                if p == 0:
                    pltpu.make_async_copy(src.at[:, cols], dst.at[mine], in_recv.at[kind, h]).start()
                else:
                    remote(src.at[:, cols], dst.at[mine], in_send.at[kind, h], in_recv.at[kind, h], at_rank(p))

    fetch(0, 0)
    fetch(1, 0)
    fetch(0, 1)
    fetch(1, 1)

    get_o.wait()
    get_g.wait()
    lane = lax.broadcasted_iota(jnp.int32, (ROWS, HD), 1)
    delta = jnp.zeros((ROWS, HD), f32)
    for r in range(RANKS):
        for h in range(HEADS):
            cols = pl.ds((r * HEADS + h) * HD, HD)
            prod = o_loc[:, cols].astype(f32) * g_loc[:, cols].astype(f32)
            total = jnp.sum(prod, axis=1, keepdims=True)
            delta = jnp.where(lane == r * 8 + h, total, delta)
    flipped = delta.T
    for r in range(RANKS):
        dl_src[r] = flipped[r * 8 : (r + 1) * 8]
    for p in range(RANKS):
        if p == 0:
            pltpu.make_async_copy(dl_src.at[x], dl.at[:, mine], dl_recv).start()
        else:
            remote(dl_src.at[rank(p)], dl.at[:, mine], dl_send, dl_recv, at_rank(p))

    here = clip_in[c]
    lse = lse_in[...] * LOG2E
    lse3[0] = lse
    for j in (1, 2):
        seen = jnp.logical_and(clip_in[lax.max(c - j, 0)] == here, c >= j)
        lse3[j] = jnp.where(seen, lse, HIDDEN)
    arrived(dl, dl_recv)

    def give(h):
        arrived(kv.at[0, h], in_recv.at[0, h])
        remote(kv.at[0, h], kv.at[1, h], kv_send.at[0, h], kv_recv.at[0, h], at_ctx(1))

        @pl.when(even)
        def _():
            remote(kv.at[0, h], kv.at[2, h], kv_send.at[1, h], kv_recv.at[1, h], at_ctx(2))

    def grads(h, j):
        key = kv[j, h, 0]
        value = kv[j, h, 1]
        dk = jnp.zeros((GROUP, HD), f32)
        dv = jnp.zeros((GROUP, HD), f32)
        for t in range(GROUP // BQ):
            rows = pl.ds(t * BQ, BQ)
            query = qg[h, 0, rows]
            grad = qg[h, 1, rows]
            score = dot(key, query, 1, 1)
            prob = jnp.exp2(score * (SCALE * LOG2E) - lse3[j, pl.ds(h, 1), rows])
            dprob = dot(value, grad, 1, 1)
            dscore = (prob * (dprob - dl[pl.ds(h, 1), rows])).astype(bf16)
            dv += dot(prob.astype(bf16), grad, 1, 0)
            dk += dot(dscore, query, 1, 0)
            step = dot(dscore, key, 0, 0)
            if j == 0:
                dq[h, rows] = step
            elif j == 1:
                dq[h, rows] += step
            else:
                stage[0, h, rows] = ((dq[h, rows] + step) * SCALE).astype(bf16)
        if j == 0:
            own[h, 0] = dk
            own[h, 1] = dv
        else:
            part[j - 1, h, 0] = dk.astype(bf16)
            part[j - 1, h, 1] = dv.astype(bf16)

    def put(which, out, h):
        cols = pl.ds(pl.multiple_of((x * HEADS + h) * HD, HD), HD)
        for p in (1, 3, 2, 0):
            src = stage.at[which, h, pl.ds(pl.multiple_of(rank(p) * ROWS, ROWS), ROWS)]
            if p == 0:
                pltpu.make_async_copy(src, out.at[:, cols], out_recv.at[which]).start()
            else:
                remote(src, out.at[:, cols], out_send.at[which, h], out_recv.at[which], at_rank(p))

    give(0)

    def step(i, _):
        @pl.when(i < HEADS)
        def _():
            arrived(qg.at[i], in_recv.at[1, i])

        @pl.when(i + 2 < HEADS)
        def _():
            fetch(0, i + 2)

        @pl.when(i < HEADS)
        def _():
            grads(i, 0)

        @pl.when(i + 1 < HEADS)
        def _():
            give(i + 1)

        @pl.when(i + 2 < HEADS)
        def _():
            fetch(1, i + 2)

        inner = jnp.logical_and(i >= 1, i <= HEADS)

        @pl.when(inner)
        def _():
            h = i - 1
            arrived(kv.at[1, h], kv_recv.at[0, h])

            @pl.when(even)
            def _():
                remote(kv.at[1, h], kv.at[2, h], kv_send.at[2, h], kv_recv.at[1, h], at_ctx(1))

            grads(h, 1)

            @pl.when(odd)
            def _():
                remote(part.at[0, h], back1.at[h], part_send.at[0, h], back_recv.at[0, h], at_ctx(-1))

            arrived(kv.at[2, h], kv_recv.at[1, h])
            grads(h, 2)

            @pl.when(odd)
            def _():
                remote(part.at[1, h], relay.at[h], part_send.at[1, h], relay_recv.at[h], at_ctx(-1))

            @pl.when(even)
            def _():
                remote(part.at[1, h], back2.at[h], part_send.at[1, h], back_recv.at[1, h], at_ctx(-2))

            put(0, q_out, h)

        @pl.when(i >= 2)
        def _():
            h = i - 2
            arrived(back1.at[h], back_recv.at[0, h])

            @pl.when(even)
            def _():
                arrived(back2.at[h], back_recv.at[1, h])
                dk = own[h, 0] + back1[h, 0].astype(f32) + back2[h, 0].astype(f32)
                dv = own[h, 1] + back1[h, 1].astype(f32) + back2[h, 1].astype(f32)
                stage[1, h] = (dk * SCALE).astype(bf16)
                stage[2, h] = dv.astype(bf16)

            @pl.when(odd)
            def _():
                stage[1, h] = ((own[h, 0] + back1[h, 0].astype(f32)) * SCALE).astype(bf16)
                stage[2, h] = (own[h, 1] + back1[h, 1].astype(f32)).astype(bf16)

            put(1, k_out, h)
            put(2, v_out, h)

        @pl.when(jnp.logical_and(inner, even))
        def _():
            h = i - 1
            arrived(relay.at[h], relay_recv.at[h])
            for n in range(2):
                part[0, h, n] = (part[0, h, n].astype(f32) + relay[h, n].astype(f32)).astype(bf16)
            remote(part.at[0, h], back1.at[h], part_send.at[0, h], back_recv.at[0, h], at_ctx(-1))

        return 0

    lax.fori_loop(0, HEADS + 2, step, 0)

    most = pl.ds(0, GROUP - ROWS)
    for r in range(1, RANKS):
        arrived(dl_src.at[r], dl_send)

    def drain(h, _):
        arrived(kv.at[0, h, :, most], in_send.at[0, h])
        arrived(qg.at[h, :, most], in_send.at[1, h])
        arrived(kv.at[0, h], kv_send.at[0, h])
        arrived(part.at[0, h], part_send.at[0, h])
        arrived(part.at[1, h], part_send.at[1, h])
        for n in range(3):
            arrived(stage.at[n, h, most], out_send.at[n, h])

        @pl.when(even)
        def _():
            arrived(kv.at[0, h], kv_send.at[1, h])
            arrived(kv.at[1, h], kv_send.at[2, h])

        return 0

    lax.fori_loop(0, HEADS, drain, 0)
    arrived(q_out, out_recv.at[0])
    arrived(k_out, out_recv.at[1])
    arrived(v_out, out_recv.at[2])


def local(queries, keys, values, outputs, out_grad, logsumexp, clip_of_group):
    hbm = pl.BlockSpec(memory_space=pl.ANY)
    vmem = pl.BlockSpec(memory_space=pltpu.VMEM)
    smem = pl.BlockSpec(memory_space=pltpu.SMEM)
    dma = pltpu.SemaphoreType.DMA
    whole = (2, GROUP, HD)
    out = jax.ShapeDtypeStruct((ROWS, RANKS * HEADS * HD), bf16)
    return pl.pallas_call(
        kernel,
        out_shape=(out, out, out),
        in_specs=[hbm, hbm, hbm, hbm, hbm, vmem, smem],
        out_specs=(hbm, hbm, hbm),
        scratch_shapes=[
            pltpu.VMEM((HEADS, *whole), bf16),
            pltpu.VMEM((3, HEADS, *whole), bf16),
            pltpu.VMEM((HEADS, *whole), f32),
            pltpu.VMEM((HEADS, GROUP, HD), f32),
            pltpu.VMEM((2, HEADS, *whole), bf16),
            pltpu.VMEM((HEADS, *whole), bf16),
            pltpu.VMEM((HEADS, *whole), bf16),
            pltpu.VMEM((HEADS, *whole), bf16),
            pltpu.VMEM((3, HEADS, GROUP, HD), bf16),
            pltpu.VMEM((ROWS, RANKS * HEADS * HD), bf16),
            pltpu.VMEM((ROWS, RANKS * HEADS * HD), bf16),
            pltpu.VMEM((RANKS, 8, ROWS), f32),
            pltpu.VMEM((8, GROUP), f32),
            pltpu.VMEM((3, HEADS, GROUP), f32),
            dma((2, HEADS)),
            dma((2, HEADS)),
            dma((3, HEADS)),
            dma((2, HEADS)),
            dma((2, HEADS)),
            dma((HEADS,)),
            dma((2, HEADS)),
            dma((3, HEADS)),
            dma((3,)),
            dma,
            dma,
            dma((2,)),
        ],
        cost_estimate=pl.CostEstimate(
            flops=2 * 5 * 3 * HEADS * GROUP * GROUP * HD,
            bytes_accessed=12 * 2**20,
            transcendentals=3 * HEADS * GROUP * GROUP,
        ),
        compiler_params=pltpu.CompilerParams(
            collective_id=0, has_side_effects=True, vmem_limit_bytes=58 * 2**20
        ),
        name="clip_attention_backward",
    )(queries, keys, values, outputs, out_grad, logsumexp, clip_of_group)


def solution(mesh):
    rows = P(("ctx", "head"), None)
    return jax.shard_map(
        local,
        mesh=mesh,
        in_specs=(rows, rows, rows, rows, rows, P("head", "ctx"), P()),
        out_specs=(rows, rows, rows),
        check_vma=False,
    )
```

```python
import jax
import jax.numpy as jnp
from jax import lax
from jax.experimental import pallas as pl
from jax.experimental.pallas import tpu as pltpu
from jax.sharding import PartitionSpec as P

HD = 128
GROUP = 1024
HEADS = 6
RANKS = 4
COUNT = 32
ROWS = GROUP // RANKS
KEYS = 2 * ROWS
BQ = 1024
AHEAD = 2
HOLD = 5
HOLD_DQ = 4
MESH = pl.DeviceIdType.MESH
SCALE = HD**-0.5
LOG2E = 1.4426950408889634
HIDDEN = 1e30
f32, bf16 = jnp.float32, jnp.bfloat16


def dot(a, b, ca, cb):
    return lax.dot_general(a, b, (((ca,), (cb,)), ((), ())), preferred_element_type=f32)


def kernel(
    q_in, k_in, v_in, o_in, g_in, lse_in, clip_in,
    q_out, k_out, v_out,
    qg, kv, own, dq, dq_away, dq_in, part, relay, back1, back2, stage, o_loc, g_loc, dl_src, dl, lse_far, lse3,
    in_send, kv_in, outer_in, q_in_sem, fwd_send, kv_send, kv_recv, part_send, relay_recv, back_recv,
    dq_send, dq_recv, out_send, out_recv, dl_send, dl_recv, loc,
):
    x = lax.axis_index("head")
    c = lax.axis_index("ctx")
    even = lax.rem(c, 2) == 0
    odd = lax.rem(c, 2) == 1

    def rank(p):
        return lax.rem(x + p + RANKS, RANKS)

    def at_rank(p):
        return {"head": rank(p)}

    def at_ctx(d):
        return {"ctx": lax.rem(c + d + COUNT, COUNT)}

    def arrived(ref, sem):
        pltpu.make_async_copy(ref, ref, sem).wait()

    def remote(src, dst, send, recv, device):
        pltpu.make_async_remote_copy(
            src_ref=src, dst_ref=dst, send_sem=send, recv_sem=recv,
            device_id=device, device_id_type=MESH,
        ).start()

    def block(p):
        return pl.ds(pl.multiple_of(rank(p) * ROWS, ROWS), ROWS)

    def head_cols(p, h):
        return pl.ds(pl.multiple_of((rank(p) * HEADS + h) * HD, HD), HD)

    SIDE = (1, -1)
    SET = (0, -1)
    NEAR, FAR = pl.ds(0, ROWS), pl.ds(ROWS, ROWS)

    get_o = pltpu.make_async_copy(o_in, o_loc, loc.at[0])
    get_g = pltpu.make_async_copy(g_in, g_loc, loc.at[1])
    get_o.start()
    get_g.start()

    barrier = pltpu.get_barrier_semaphore()
    for p in range(1, RANKS):
        pl.semaphore_signal(barrier, inc=1, device_id=at_rank(p), device_id_type=MESH)
    for d in (-2, -1, 1, 2):
        pl.semaphore_signal(barrier, inc=1, device_id=at_ctx(d), device_id_type=MESH)
    pl.semaphore_wait(barrier, RANKS - 1 + 4)

    def fetch_outer(h):
        for role in (0, 1):
            side = SIDE[role]
            cols = head_cols(side + SET[role], h)
            for n, src in ((0, q_in), (1, g_in)):
                remote(src.at[:, cols], qg.at[h, role, n, block(0)], in_send.at[h], outer_in.at[h], at_rank(side))
        for role in (0, 1):
            side = SIDE[role]
            cols = head_cols(side + SET[role], h)
            for n, src in ((0, k_in), (1, v_in)):
                remote(src.at[:, cols], kv.at[0, h, role, n, FAR], in_send.at[h], kv_in.at[h], at_rank(side))
        for role in (0, 1):
            cols = head_cols(SET[role], h)
            for n, src in ((0, k_in), (1, v_in)):
                pltpu.make_async_copy(src.at[:, cols], kv.at[0, h, role, n, NEAR], kv_in.at[h]).start()

    def fetch_own(h):
        for role in (0, 1):
            cols = head_cols(SET[role], h)
            for n, src in ((0, q_in), (1, g_in)):
                remote(
                    src.at[:, cols], qg.at[h, 1 - role, n, block(0)],
                    in_send.at[h], q_in_sem.at[h], at_rank(SIDE[role]),
                )
                pltpu.make_async_copy(src.at[:, cols], qg.at[h, role, n, block(0)], q_in_sem.at[h]).start()

    def forward(h):
        arrived(qg.at[h, :, :, NEAR], outer_in.at[h])
        for role in (0, 1):
            outer = block(-SIDE[role])
            remote(
                qg.at[h, role, :, outer], qg.at[h, 1 - role, :, outer],
                fwd_send.at[h], q_in_sem.at[h], at_rank(SIDE[role]),
            )

    def give(h):
        arrived(kv.at[0, h], kv_in.at[h])
        remote(kv.at[0, h], kv.at[1, h], kv_send.at[0, h], kv_recv.at[0, h], at_ctx(1))

        @pl.when(even)
        def _():
            remote(kv.at[0, h], kv.at[2, h], kv_send.at[1, h], kv_recv.at[1, h], at_ctx(2))

    for h in range(AHEAD):
        fetch_outer(h)
        fetch_own(h)
    remote(lse_in, lse_far, dl_send.at[0], dl_recv.at[0], at_rank(1))

    get_o.wait()
    get_g.wait()
    lane = lax.broadcasted_iota(jnp.int32, (ROWS, HD), 1)
    delta = jnp.zeros((ROWS, HD), f32)
    for r in range(RANKS):
        for h in range(HEADS):
            cols = pl.ds((r * HEADS + h) * HD, HD)
            prod = o_loc[:, cols].astype(f32) * g_loc[:, cols].astype(f32)
            total = jnp.sum(prod, axis=1, keepdims=True)
            delta = jnp.where(lane == r * 8 + h, total, delta)
    flipped = delta.T
    for r in range(RANKS):
        dl_src[r] = flipped[r * 8 : (r + 1) * 8]
    for role in (0, 1):
        for p in range(RANKS):
            src, dst = dl_src.at[rank(p + SET[role])], dl.at[role, :, block(0)]
            if p == 0:
                pltpu.make_async_copy(src, dst, dl_recv.at[1]).start()
            else:
                remote(src, dst, dl_send.at[1], dl_recv.at[1], at_rank(p))

    give(0)
    forward(0)

    arrived(lse_far, dl_recv.at[0])
    here = clip_in[c]
    for role, src in ((0, lse_in), (1, lse_far)):
        lse = src[...] * LOG2E
        lse3[role, 0] = lse
        for j in (1, 2):
            seen = jnp.logical_and(clip_in[lax.max(c - j, 0)] == here, c >= j)
            lse3[role, j] = jnp.where(seen, lse, HIDDEN)
    arrived(dl, dl_recv.at[1])

    def grads(h, j):
        def one(role, _):
            key = kv[j, h, role, 0]
            value = kv[j, h, role, 1]
            dk = jnp.zeros((KEYS, HD), f32)
            dv = jnp.zeros((KEYS, HD), f32)
            for t in range(GROUP // BQ):
                rows = pl.ds(t * BQ, BQ)
                query = qg[h, role, 0, rows]
                grad = qg[h, role, 1, rows]
                score = dot(key, query, 1, 1)
                prob = jnp.exp2(score * (SCALE * LOG2E) - lse3[role, j, pl.ds(h, 1), rows])
                dprob = dot(value, grad, 1, 1)
                dscore = (prob * (dprob - dl[role, pl.ds(h, 1), rows])).astype(bf16)
                dv += dot(prob.astype(bf16), grad, 1, 0)
                dk += dot(dscore, query, 1, 0)
                step = dot(key, dscore, 0, 0)
                if j == 0:
                    dq[h, role, :, rows] = step
                else:
                    dq[h, role, :, rows] += step
            if j == 0:
                own[h, role, 0] = dk
                own[h, role, 1] = dv
            else:
                part[j - 1, h, role, 0] = dk.astype(bf16)
                part[j - 1, h, role, 1] = dv.astype(bf16)
            return 0

        lax.fori_loop(0, 2, one, 0)

    def put(which, out, h):
        for role in (0, 1):
            cols = head_cols(SET[role], h)
            remote(
                stage.at[which, h, role, FAR], out.at[:, cols],
                out_send.at[which, h], out_recv.at[which], at_rank(-SIDE[role]),
            )
            pltpu.make_async_copy(stage.at[which, h, role, NEAR], out.at[:, cols], out_recv.at[which]).start()

    def share_dq(h):
        for role in (0, 1):
            dq_away[h, role, NEAR] = dq[h, role, :, block(SIDE[role])].T.astype(bf16)
            dq_away[h, role, FAR] = dq[h, role, :, block(2)].T.astype(bf16)
            remote(dq_away.at[h, role], dq_in.at[h, 1 - role], dq_send.at[h], dq_recv.at[h], at_rank(SIDE[role]))

    def finish_dq(h):
        arrived(dq_in.at[h], dq_recv.at[h])
        for role in (0, 1):
            for where, p in ((NEAR, 0), (FAR, -SIDE[role])):
                total = dq[h, role, :, block(p)].T + dq_in[h, role, where].astype(f32)
                stage[0, h, role, where] = (total * SCALE).astype(bf16)
        put(0, q_out, h)

    def finish_kv(h):
        arrived(back1.at[h], back_recv.at[0, h])

        @pl.when(even)
        def _():
            arrived(back2.at[h], back_recv.at[1, h])
            for n, factor in ((0, SCALE), (1, 1.0)):
                for role in (0, 1):
                    total = own[h, role, n] + back1[h, role, n].astype(f32) + back2[h, role, n].astype(f32)
                    stage[1 + n, h, role] = (total * factor).astype(bf16)

        @pl.when(odd)
        def _():
            for n, factor in ((0, SCALE), (1, 1.0)):
                for role in (0, 1):
                    total = own[h, role, n] + back1[h, role, n].astype(f32)
                    stage[1 + n, h, role] = (total * factor).astype(bf16)

    def put_kv(h):
        put(1, k_out, h)
        put(2, v_out, h)

    def later(i, first, lag, do):
        @pl.when(i == first)
        def _():
            def each(h, _):
                do(h)
                return 0

            lax.fori_loop(0, first - lag + 1, each, 0)

        @pl.when(jnp.logical_and(i > first, i - lag < HEADS))
        def _():
            do(i - lag)

    def step(i, _):
        @pl.when(i + AHEAD < HEADS)
        def _():
            fetch_outer(i + AHEAD)

        @pl.when(i < HEADS)
        def _():
            arrived(qg.at[i, :, :, pl.ds(0, GROUP - ROWS)], q_in_sem.at[i])
            grads(i, 0)

        @pl.when(i + 1 < HEADS)
        def _():
            give(i + 1)
            forward(i + 1)

        @pl.when(i + AHEAD < HEADS)
        def _():
            fetch_own(i + AHEAD)

        inner = jnp.logical_and(i >= 1, i <= HEADS)

        @pl.when(inner)
        def _():
            h = i - 1
            arrived(kv.at[1, h], kv_recv.at[0, h])

            @pl.when(even)
            def _():
                remote(kv.at[1, h], kv.at[2, h], kv_send.at[2, h], kv_recv.at[1, h], at_ctx(1))

            grads(h, 1)

            @pl.when(odd)
            def _():
                remote(part.at[0, h], back1.at[h], part_send.at[0, h], back_recv.at[0, h], at_ctx(-1))

            arrived(kv.at[2, h], kv_recv.at[1, h])
            grads(h, 2)

            @pl.when(odd)
            def _():
                remote(part.at[1, h], relay.at[h], part_send.at[1, h], relay_recv.at[h], at_ctx(-1))

            @pl.when(even)
            def _():
                remote(part.at[1, h], back2.at[h], part_send.at[1, h], back_recv.at[1, h], at_ctx(-2))

        later(i, HOLD_DQ, 1, share_dq)

        @pl.when(i >= 2)
        def _():
            finish_kv(i - 2)

        later(i, HOLD, 2, put_kv)
        later(i, HOLD, 2, finish_dq)

        @pl.when(jnp.logical_and(inner, even))
        def _():
            h = i - 1
            arrived(relay.at[h], relay_recv.at[h])
            for role in (0, 1):
                for n in (0, 1):
                    total = part[0, h, role, n].astype(f32) + relay[h, role, n].astype(f32)
                    part[0, h, role, n] = total.astype(bf16)
            remote(part.at[0, h], back1.at[h], part_send.at[0, h], back_recv.at[0, h], at_ctx(-1))

        return 0

    lax.fori_loop(0, HEADS + 2, step, 0)

    arrived(lse_in, dl_send.at[0])
    for r in range(1, RANKS):
        arrived(dl_src.at[pl.ds(0, 2)], dl_send.at[1])

    def drain(h, _):
        arrived(qg.at[h, :, :, pl.ds(0, GROUP - ROWS)], in_send.at[h])
        arrived(qg.at[h, :, :, NEAR], fwd_send.at[h])
        arrived(kv.at[0, h], kv_send.at[0, h])
        arrived(part.at[0, h], part_send.at[0, h])
        arrived(part.at[1, h], part_send.at[1, h])
        arrived(dq_away.at[h], dq_send.at[h])
        for n in range(3):
            arrived(stage.at[n, h, :, NEAR], out_send.at[n, h])

        @pl.when(even)
        def _():
            arrived(kv.at[0, h], kv_send.at[1, h])
            arrived(kv.at[1, h], kv_send.at[2, h])

        return 0

    lax.fori_loop(0, HEADS, drain, 0)
    arrived(q_out, out_recv.at[0])
    arrived(k_out, out_recv.at[1])
    arrived(v_out, out_recv.at[2])


def local(queries, keys, values, outputs, out_grad, logsumexp, clip_of_group):
    hbm = pl.BlockSpec(memory_space=pl.ANY)
    vmem = pl.BlockSpec(memory_space=pltpu.VMEM)
    smem = pl.BlockSpec(memory_space=pltpu.SMEM)
    dma = pltpu.SemaphoreType.DMA
    half = (HEADS, 2, 2, KEYS, HD)
    out = jax.ShapeDtypeStruct((ROWS, RANKS * HEADS * HD), bf16)
    return pl.pallas_call(
        kernel,
        out_shape=(out, out, out),
        in_specs=[hbm, hbm, hbm, hbm, hbm, vmem, smem],
        out_specs=(hbm, hbm, hbm),
        scratch_shapes=[
            pltpu.VMEM((HEADS, 2, 2, GROUP, HD), bf16),
            pltpu.VMEM((3, *half), bf16),
            pltpu.VMEM(half, f32),
            pltpu.VMEM((HEADS, 2, HD, GROUP), f32),
            pltpu.VMEM((HEADS, 2, KEYS, HD), bf16),
            pltpu.VMEM((HEADS, 2, KEYS, HD), bf16),
            pltpu.VMEM((2, *half), bf16),
            pltpu.VMEM(half, bf16),
            pltpu.VMEM(half, bf16),
            pltpu.VMEM(half, bf16),
            pltpu.VMEM((3, HEADS, 2, KEYS, HD), bf16),
            pltpu.VMEM((ROWS, RANKS * HEADS * HD), bf16),
            pltpu.VMEM((ROWS, RANKS * HEADS * HD), bf16),
            pltpu.VMEM((RANKS, 8, ROWS), f32),
            pltpu.VMEM((2, 8, GROUP), f32),
            pltpu.VMEM((HEADS, GROUP), f32),
            pltpu.VMEM((2, 3, HEADS, GROUP), f32),
            dma((HEADS,)),
            dma((HEADS,)),
            dma((HEADS,)),
            dma((HEADS,)),
            dma((HEADS,)),
            dma((3, HEADS)),
            dma((2, HEADS)),
            dma((2, HEADS)),
            dma((HEADS,)),
            dma((2, HEADS)),
            dma((HEADS,)),
            dma((HEADS,)),
            dma((3, HEADS)),
            dma((3,)),
            dma((2,)),
            dma((2,)),
            dma((2,)),
        ],
        cost_estimate=pl.CostEstimate(
            flops=2 * 5 * 3 * HEADS * GROUP * GROUP * HD,
            bytes_accessed=12 * 2**20,
            transcendentals=3 * HEADS * GROUP * GROUP,
        ),
        compiler_params=pltpu.CompilerParams(
            collective_id=0, has_side_effects=True, vmem_limit_bytes=60 * 2**20
        ),
        name="clip_attention_backward",
    )(queries, keys, values, outputs, out_grad, logsumexp, clip_of_group)


def solution(mesh):
    rows = P(("ctx", "head"), None)
    return jax.shard_map(
        local,
        mesh=mesh,
        in_specs=(rows, rows, rows, rows, rows, P("head", "ctx"), P()),
        out_specs=(rows, rows, rows),
        check_vma=False,
    )
```

```python
import jax
import jax.numpy as jnp
from jax import lax
from jax.experimental import pallas as pl
from jax.experimental.pallas import tpu as pltpu
from jax.sharding import PartitionSpec as P

HD = 128
GROUP = 1024
HEADS = 6
RANKS = 4
COUNT = 32
ROWS = GROUP // RANKS
KEYS = 2 * ROWS
BQ = 1024
AHEAD = 2
HOLD = 5
EARLY = 3
MESH = pl.DeviceIdType.MESH
SCALE = HD**-0.5
LOG2E = 1.4426950408889634
HIDDEN = 1e30
f32, bf16 = jnp.float32, jnp.bfloat16


def dot(a, b, ca, cb):
    return lax.dot_general(a, b, (((ca,), (cb,)), ((), ())), preferred_element_type=f32)


def kernel(
    q_in, k_in, v_in, o_in, g_in, lse_in, clip_in,
    q_out, k_out, v_out,
    qg, kv, own, dq, dq_in, part, relay, back1, back2, stage, dl_src, dl, lse_far, lse3,
    in_send, kv_in, outer_in, q_in_sem, fwd_send, kv_send, kv_recv, part_send, relay_recv, back_recv,
    dq_send, dq_recv, out_send, out_recv, dl_send, dl_recv, loc,
):
    x = lax.axis_index("head")
    c = lax.axis_index("ctx")
    even = lax.rem(c, 2) == 0
    odd = lax.rem(c, 2) == 1

    def rank(p):
        return lax.rem(x + p + RANKS, RANKS)

    def at_rank(p):
        return {"head": rank(p)}

    def at_ctx(d):
        return {"ctx": lax.rem(c + d + COUNT, COUNT)}

    def arrived(ref, sem):
        pltpu.make_async_copy(ref, ref, sem).wait()

    def remote(src, dst, send, recv, device):
        pltpu.make_async_remote_copy(
            src_ref=src, dst_ref=dst, send_sem=send, recv_sem=recv,
            device_id=device, device_id_type=MESH,
        ).start()

    def block(p):
        return pl.ds(pl.multiple_of(rank(p) * ROWS, ROWS), ROWS)

    def head_cols(p, h):
        return pl.ds(pl.multiple_of((rank(p) * HEADS + h) * HD, HD), HD)

    SIDE = (1, -1)
    SET = (0, -1)
    NEAR, FAR = pl.ds(0, ROWS), pl.ds(ROWS, ROWS)

    barrier = pltpu.get_barrier_semaphore()
    for p in range(1, RANKS):
        pl.semaphore_signal(barrier, inc=1, device_id=at_rank(p), device_id_type=MESH)
    for d in (-2, -1, 1, 2):
        pl.semaphore_signal(barrier, inc=1, device_id=at_ctx(d), device_id_type=MESH)

    def load(h, _):
        for r in range(RANKS):
            cols = pl.ds(pl.multiple_of((r * HEADS + h) * HD, HD), HD)
            pltpu.make_async_copy(o_in.at[:, cols], stage.at[r // 2, h, r % 2, NEAR], loc).start()
            pltpu.make_async_copy(g_in.at[:, cols], stage.at[r // 2, h, r % 2, FAR], loc).start()
        return 0

    lax.fori_loop(0, HEADS, load, 0)
    pl.semaphore_wait(barrier, RANKS - 1 + 4)

    def fetch_outer(h):
        for role in (0, 1):
            side = SIDE[role]
            cols = head_cols(side + SET[role], h)
            for n, src in ((0, q_in), (1, g_in)):
                remote(src.at[:, cols], qg.at[h, role, n, block(0)], in_send.at[h], outer_in.at[h], at_rank(side))
        for role in (0, 1):
            side = SIDE[role]
            cols = head_cols(side + SET[role], h)
            for n, src in ((0, k_in), (1, v_in)):
                remote(src.at[:, cols], kv.at[0, h, role, n, FAR], in_send.at[h], kv_in.at[h], at_rank(side))
        for role in (0, 1):
            cols = head_cols(SET[role], h)
            for n, src in ((0, k_in), (1, v_in)):
                pltpu.make_async_copy(src.at[:, cols], kv.at[0, h, role, n, NEAR], kv_in.at[h]).start()

    def fetch_own(h):
        for role in (0, 1):
            cols = head_cols(SET[role], h)
            for n, src in ((0, q_in), (1, g_in)):
                remote(
                    src.at[:, cols], qg.at[h, 1 - role, n, block(0)],
                    in_send.at[h], q_in_sem.at[h], at_rank(SIDE[role]),
                )
                pltpu.make_async_copy(src.at[:, cols], qg.at[h, role, n, block(0)], q_in_sem.at[h]).start()

    def forward(h):
        arrived(qg.at[h, :, :, NEAR], outer_in.at[h])
        for role in (0, 1):
            outer = block(-SIDE[role])
            remote(
                qg.at[h, role, :, outer], qg.at[h, 1 - role, :, outer],
                fwd_send.at[h], q_in_sem.at[h], at_rank(SIDE[role]),
            )

    def give(h):
        arrived(kv.at[0, h], kv_in.at[h])
        remote(kv.at[0, h], kv.at[1, h], kv_send.at[0, h], kv_recv.at[0, h], at_ctx(1))

        @pl.when(even)
        def _():
            remote(kv.at[0, h], kv.at[2, h], kv_send.at[1, h], kv_recv.at[1, h], at_ctx(2))

    fetch_outer(0)
    fetch_own(0)
    remote(lse_in, lse_far, dl_send.at[0], dl_recv.at[0], at_rank(1))

    arrived(stage.at[pl.ds(0, 2)], loc)
    lane = lax.broadcasted_iota(jnp.int32, (ROWS, HD), 1)
    delta = jnp.zeros((ROWS, HD), f32)
    for r in range(RANKS):
        for h in range(HEADS):
            prod = stage[r // 2, h, r % 2, NEAR].astype(f32) * stage[r // 2, h, r % 2, FAR].astype(f32)
            total = jnp.sum(prod, axis=1, keepdims=True)
            delta = jnp.where(lane == r * 8 + h, total, delta)
    flipped = delta.T
    for r in range(RANKS):
        dl_src[r] = flipped[r * 8 : (r + 1) * 8]
    for role in (0, 1):
        for p in range(RANKS):
            src, dst = dl_src.at[rank(p + SET[role])], dl.at[role, :, block(0)]
            if p == 0:
                pltpu.make_async_copy(src, dst, dl_recv.at[1]).start()
            else:
                remote(src, dst, dl_send.at[1], dl_recv.at[1], at_rank(p))

    fetch_outer(1)
    forward(0)
    give(0)
    fetch_own(1)

    arrived(lse_far, dl_recv.at[0])
    here = clip_in[c]
    for role, src in ((0, lse_in), (1, lse_far)):
        lse = src[...] * LOG2E
        lse3[role, 0] = lse
        for j in (1, 2):
            seen = jnp.logical_and(clip_in[lax.max(c - j, 0)] == here, c >= j)
            lse3[role, j] = jnp.where(seen, lse, HIDDEN)
    arrived(dl, dl_recv.at[1])

    def grads(h, j):
        def one(role, _):
            key = kv[j, h, role, 0]
            value = kv[j, h, role, 1]
            dk = jnp.zeros((KEYS, HD), f32)
            dv = jnp.zeros((KEYS, HD), f32)
            for t in range(GROUP // BQ):
                rows = pl.ds(t * BQ, BQ)
                query = qg[h, role, 0, rows]
                grad = qg[h, role, 1, rows]
                score = dot(key, query, 1, 1)
                prob = jnp.exp2(score * (SCALE * LOG2E) - lse3[role, j, pl.ds(h, 1), rows])
                dprob = dot(value, grad, 1, 1)
                dscore = (prob * (dprob - dl[role, pl.ds(h, 1), rows])).astype(bf16)
                dv += dot(prob.astype(bf16), grad, 1, 0)
                dk += dot(dscore, query, 1, 0)
                step = dot(key, dscore, 0, 0)
                if j == 0:
                    dq[h, role, :, rows] = step
                else:
                    dq[h, role, :, rows] += step
            if j == 0:
                own[h, role, 0] = dk
                own[h, role, 1] = dv
            else:
                part[j - 1, h, role, 0] = dk.astype(bf16)
                part[j - 1, h, role, 1] = dv.astype(bf16)

        one(0, 0)
        one(1, 0)

    def put(which, out, h):
        for role in (0, 1):
            cols = head_cols(SET[role], h)
            remote(
                stage.at[which, h, role, FAR], out.at[:, cols],
                out_send.at[which, h], out_recv.at[which], at_rank(-SIDE[role]),
            )
            pltpu.make_async_copy(stage.at[which, h, role, NEAR], out.at[:, cols], out_recv.at[which]).start()

    def share_dq(h):
        for role in (0, 1):
            stage[0, h, role, NEAR] = dq[h, role, :, block(SIDE[role])].T.astype(bf16)
            stage[0, h, role, FAR] = dq[h, role, :, block(2)].T.astype(bf16)
            remote(stage.at[0, h, role], dq_in.at[h, 1 - role], dq_send.at[h], dq_recv.at[h], at_rank(SIDE[role]))

    def finish_dq(h):
        arrived(dq_in.at[h], dq_recv.at[h])
        arrived(stage.at[0, h], dq_send.at[h])
        for role in (0, 1):
            for where, p in ((NEAR, 0), (FAR, -SIDE[role])):
                total = dq[h, role, :, block(p)].T + dq_in[h, role, where].astype(f32)
                stage[0, h, role, where] = (total * SCALE).astype(bf16)
        put(0, q_out, h)

    def finish_kv(h):
        arrived(back1.at[h], back_recv.at[0, h])

        @pl.when(even)
        def _():
            arrived(back2.at[h], back_recv.at[1, h])
            for n, factor in ((0, SCALE), (1, 1.0)):
                for role in (0, 1):
                    total = own[h, role, n] + back1[h, role, n].astype(f32) + back2[h, role, n].astype(f32)
                    stage[1 + n, h, role] = (total * factor).astype(bf16)

        @pl.when(odd)
        def _():
            for n, factor in ((0, SCALE), (1, 1.0)):
                for role in (0, 1):
                    total = own[h, role, n] + back1[h, role, n].astype(f32)
                    stage[1 + n, h, role] = (total * factor).astype(bf16)

    def put_kv(h):
        put(1, k_out, h)
        put(2, v_out, h)

    def several(first, last, do):
        def each(h, _):
            do(h)
            return 0

        lax.fori_loop(first, last, each, 0)

    def step(i, _):
        @pl.when(i + AHEAD < HEADS)
        def _():
            fetch_outer(i + AHEAD)

        @pl.when(i < HEADS)
        def _():
            arrived(qg.at[i, :, :, pl.ds(0, GROUP - ROWS)], q_in_sem.at[i])

        @pl.when(i == HOLD)
        def _():
            several(0, HOLD - 2, put_kv)
            several(EARLY, HOLD - 1, share_dq)

        @pl.when(i < HEADS)
        def _():
            grads(i, 0)

        @pl.when(i + 1 < HEADS)
        def _():
            give(i + 1)
            forward(i + 1)

        @pl.when(i + AHEAD < HEADS)
        def _():
            fetch_own(i + AHEAD)

        inner = jnp.logical_and(i >= 1, i <= HEADS)

        @pl.when(inner)
        def _():
            h = i - 1
            arrived(kv.at[1, h], kv_recv.at[0, h])

            @pl.when(even)
            def _():
                remote(kv.at[1, h], kv.at[2, h], kv_send.at[2, h], kv_recv.at[1, h], at_ctx(1))

            grads(h, 1)

            @pl.when(odd)
            def _():
                remote(part.at[0, h], back1.at[h], part_send.at[0, h], back_recv.at[0, h], at_ctx(-1))

            arrived(kv.at[2, h], kv_recv.at[1, h])
            grads(h, 2)

            @pl.when(odd)
            def _():
                remote(part.at[1, h], relay.at[h], part_send.at[1, h], relay_recv.at[h], at_ctx(-1))

            @pl.when(even)
            def _():
                remote(part.at[1, h], back2.at[h], part_send.at[1, h], back_recv.at[1, h], at_ctx(-2))

        @pl.when(jnp.logical_or(i <= EARLY, i >= HOLD) & inner)
        def _():
            share_dq(i - 1)

        @pl.when(i >= 2)
        def _():
            finish_kv(i - 2)

        @pl.when(i >= HOLD)
        def _():
            put_kv(i - 2)

        @pl.when(i == HOLD)
        def _():
            several(0, HOLD - 1, finish_dq)

        @pl.when(i > HOLD)
        def _():
            finish_dq(i - 2)

        @pl.when(jnp.logical_and(inner, even))
        def _():
            h = i - 1
            arrived(relay.at[h], relay_recv.at[h])
            for role in (0, 1):
                for n in (0, 1):
                    total = part[0, h, role, n].astype(f32) + relay[h, role, n].astype(f32)
                    part[0, h, role, n] = total.astype(bf16)
            remote(part.at[0, h], back1.at[h], part_send.at[0, h], back_recv.at[0, h], at_ctx(-1))

        return 0

    lax.fori_loop(0, HEADS + 2, step, 0)

    arrived(lse_in, dl_send.at[0])
    for r in range(1, RANKS):
        arrived(dl_src.at[pl.ds(0, 2)], dl_send.at[1])

    def drain(h, _):
        arrived(qg.at[h, :, :, pl.ds(0, GROUP - ROWS)], in_send.at[h])
        arrived(qg.at[h, :, :, NEAR], fwd_send.at[h])
        arrived(kv.at[0, h], kv_send.at[0, h])
        arrived(part.at[0, h], part_send.at[0, h])
        arrived(part.at[1, h], part_send.at[1, h])
        for n in range(3):
            arrived(stage.at[n, h, :, NEAR], out_send.at[n, h])

        @pl.when(even)
        def _():
            arrived(kv.at[0, h], kv_send.at[1, h])
            arrived(kv.at[1, h], kv_send.at[2, h])

        return 0

    lax.fori_loop(0, HEADS, drain, 0)
    arrived(q_out, out_recv.at[0])
    arrived(k_out, out_recv.at[1])
    arrived(v_out, out_recv.at[2])


def local(queries, keys, values, outputs, out_grad, logsumexp, clip_of_group):
    hbm = pl.BlockSpec(memory_space=pl.ANY)
    vmem = pl.BlockSpec(memory_space=pltpu.VMEM)
    smem = pl.BlockSpec(memory_space=pltpu.SMEM)
    dma = pltpu.SemaphoreType.DMA
    half = (HEADS, 2, 2, KEYS, HD)
    out = jax.ShapeDtypeStruct((ROWS, RANKS * HEADS * HD), bf16)
    near = pltpu.VMEM((ROWS, RANKS * HEADS * HD), bf16)
    grads = pl.pallas_call(
        kernel,
        out_shape=(near, near, near),
        in_specs=[hbm, hbm, hbm, hbm, hbm, vmem, smem],
        out_specs=(hbm, hbm, hbm),
        scratch_shapes=[
            pltpu.VMEM((HEADS, 2, 2, GROUP, HD), bf16),
            pltpu.VMEM((3, *half), bf16),
            pltpu.VMEM(half, f32),
            pltpu.VMEM((HEADS, 2, HD, GROUP), f32),
            pltpu.VMEM((HEADS, 2, KEYS, HD), bf16),
            pltpu.VMEM((2, *half), bf16),
            pltpu.VMEM(half, bf16),
            pltpu.VMEM(half, bf16),
            pltpu.VMEM(half, bf16),
            pltpu.VMEM((3, HEADS, 2, KEYS, HD), bf16),
            pltpu.VMEM((RANKS, 8, ROWS), f32),
            pltpu.VMEM((2, 8, GROUP), f32),
            pltpu.VMEM((HEADS, GROUP), f32),
            pltpu.VMEM((2, 3, HEADS, GROUP), f32),
            dma((HEADS,)),
            dma((HEADS,)),
            dma((HEADS,)),
            dma((HEADS,)),
            dma((HEADS,)),
            dma((3, HEADS)),
            dma((2, HEADS)),
            dma((2, HEADS)),
            dma((HEADS,)),
            dma((2, HEADS)),
            dma((HEADS,)),
            dma((HEADS,)),
            dma((3, HEADS)),
            dma((3,)),
            dma((2,)),
            dma((2,)),
            dma,
        ],
        cost_estimate=pl.CostEstimate(
            flops=2 * 5 * 3 * HEADS * GROUP * GROUP * HD,
            bytes_accessed=12 * 2**20,
            transcendentals=3 * HEADS * GROUP * GROUP,
        ),
        compiler_params=pltpu.CompilerParams(
            collective_id=0, has_side_effects=True, vmem_limit_bytes=53 * 2**20
        ),
        name="clip_attention_backward",
    )(queries, keys, values, outputs, out_grad, logsumexp, clip_of_group)

    return grads


def solution(mesh):
    rows = P(("ctx", "head"), None)
    return jax.shard_map(
        local,
        mesh=mesh,
        in_specs=(rows, rows, rows, rows, rows, P("head", "ctx"), P()),
        out_specs=(rows, rows, rows),
        check_vma=False,
    )
```

```python
import jax
import jax.numpy as jnp
from jax import lax
from jax.experimental import pallas as pl
from jax.experimental.pallas import tpu as pltpu
from jax.sharding import PartitionSpec as P

HD = 128
GROUP = 1024
HEADS = 6
RANKS = 4
COUNT = 32
ROWS = GROUP // RANKS
KEYS = 2 * ROWS
BQ = 1024
AHEAD = 2
HOLD = 5
EARLY = 3
MESH = pl.DeviceIdType.MESH
SCALE = HD**-0.5
LOG2E = 1.4426950408889634
HIDDEN = 1e30
f32, bf16 = jnp.float32, jnp.bfloat16


def dot(a, b, ca, cb):
    return lax.dot_general(a, b, (((ca,), (cb,)), ((), ())), preferred_element_type=f32)


def kernel(
    q_in, k_in, v_in, o_in, g_in, lse_in, clip_in,
    q_out, k_out, v_out,
    qg, kv, own, dq, dq_in, part, relay, back1, back2, stage, dl_src, dl, lse_far, lse3,
    in_send, kv_in, outer_in, q_in_sem, fwd_send, kv_send, kv_recv, part_send, relay_recv, back_recv,
    dq_send, dq_recv, out_send, out_recv, dl_send, dl_recv, loc,
):
    x = lax.axis_index("head")
    c = lax.axis_index("ctx")
    even = lax.rem(c, 2) == 0
    odd = lax.rem(c, 2) == 1

    def rank(p):
        return lax.rem(x + p + RANKS, RANKS)

    def at_rank(p):
        return {"head": rank(p)}

    def at_ctx(d):
        return {"ctx": lax.rem(c + d + COUNT, COUNT)}

    def arrived(ref, sem):
        pltpu.make_async_copy(ref, ref, sem).wait()

    def remote(src, dst, send, recv, device):
        pltpu.make_async_remote_copy(
            src_ref=src, dst_ref=dst, send_sem=send, recv_sem=recv,
            device_id=device, device_id_type=MESH,
        ).start()

    def block(p):
        return pl.ds(pl.multiple_of(rank(p) * ROWS, ROWS), ROWS)

    def head_cols(p, h):
        return pl.ds(pl.multiple_of((rank(p) * HEADS + h) * HD, HD), HD)

    SIDE = (1, -1)
    SET = (0, -1)
    NEAR, FAR = pl.ds(0, ROWS), pl.ds(ROWS, ROWS)

    barrier = pltpu.get_barrier_semaphore()
    for p in range(1, RANKS):
        pl.semaphore_signal(barrier, inc=1, device_id=at_rank(p), device_id_type=MESH)
    for d in (-2, -1, 1, 2):
        pl.semaphore_signal(barrier, inc=1, device_id=at_ctx(d), device_id_type=MESH)

    def load(h, _):
        for r in range(RANKS):
            cols = pl.ds(pl.multiple_of((r * HEADS + h) * HD, HD), HD)
            pltpu.make_async_copy(o_in.at[:, cols], stage.at[r // 2, h, r % 2, NEAR], loc).start()
            pltpu.make_async_copy(g_in.at[:, cols], stage.at[r // 2, h, r % 2, FAR], loc).start()
        return 0

    lax.fori_loop(0, HEADS, load, 0)
    pl.semaphore_wait(barrier, RANKS - 1 + 4)

    def fetch_outer(h):
        for role in (0, 1):
            side = SIDE[role]
            cols = head_cols(side + SET[role], h)
            for n, src in ((0, q_in), (1, g_in)):
                remote(src.at[:, cols], qg.at[h, role, n, block(0)], in_send.at[h], outer_in.at[h], at_rank(side))

    def fetch_kv(h):
        for role in (0, 1):
            side = SIDE[role]
            cols = head_cols(side + SET[role], h)
            for n, src in ((0, k_in), (1, v_in)):
                remote(src.at[:, cols], kv.at[0, h, role, n, FAR], in_send.at[h], kv_in.at[h], at_rank(side))
        for role in (0, 1):
            cols = head_cols(SET[role], h)
            for n, src in ((0, k_in), (1, v_in)):
                pltpu.make_async_copy(src.at[:, cols], kv.at[0, h, role, n, NEAR], kv_in.at[h]).start()

    def fetch_own(h):
        for role in (0, 1):
            cols = head_cols(SET[role], h)
            for n, src in ((0, q_in), (1, g_in)):
                remote(
                    src.at[:, cols], qg.at[h, 1 - role, n, block(0)],
                    in_send.at[h], q_in_sem.at[h], at_rank(SIDE[role]),
                )
                pltpu.make_async_copy(src.at[:, cols], qg.at[h, role, n, block(0)], q_in_sem.at[h]).start()

    def forward(h):
        arrived(qg.at[h, :, :, NEAR], outer_in.at[h])
        for role in (0, 1):
            outer = block(-SIDE[role])
            remote(
                qg.at[h, role, :, outer], qg.at[h, 1 - role, :, outer],
                fwd_send.at[h], q_in_sem.at[h], at_rank(SIDE[role]),
            )

    def give(h):
        arrived(kv.at[0, h], kv_in.at[h])
        remote(kv.at[0, h], kv.at[1, h], kv_send.at[0, h], kv_recv.at[0, h], at_ctx(1))

        @pl.when(even)
        def _():
            remote(kv.at[0, h], kv.at[2, h], kv_send.at[1, h], kv_recv.at[1, h], at_ctx(2))

    fetch_kv(0)
    fetch_outer(0)
    fetch_own(0)
    fetch_kv(1)
    remote(lse_in, lse_far, dl_send.at[0], dl_recv.at[0], at_rank(1))

    arrived(stage.at[pl.ds(0, 2)], loc)
    lane = lax.broadcasted_iota(jnp.int32, (ROWS, HD), 1)
    delta = jnp.zeros((ROWS, HD), f32)
    for r in range(RANKS):
        for h in range(HEADS):
            prod = stage[r // 2, h, r % 2, NEAR].astype(f32) * stage[r // 2, h, r % 2, FAR].astype(f32)
            total = jnp.sum(prod, axis=1, keepdims=True)
            delta = jnp.where(lane == r * 8 + h, total, delta)
    flipped = delta.T
    for r in range(RANKS):
        dl_src[r] = flipped[r * 8 : (r + 1) * 8]
    for role in (0, 1):
        for p in range(RANKS):
            src, dst = dl_src.at[rank(p + SET[role])], dl.at[role, :, block(0)]
            if p == 0:
                pltpu.make_async_copy(src, dst, dl_recv.at[1]).start()
            else:
                remote(src, dst, dl_send.at[1], dl_recv.at[1], at_rank(p))

    fetch_outer(1)
    forward(0)
    give(0)
    fetch_own(1)
    fetch_kv(2)
    give(1)

    arrived(lse_far, dl_recv.at[0])
    here = clip_in[c]
    for role, src in ((0, lse_in), (1, lse_far)):
        lse = src[...] * LOG2E
        lse3[role, 0] = lse
        for j in (1, 2):
            seen = jnp.logical_and(clip_in[lax.max(c - j, 0)] == here, c >= j)
            lse3[role, j] = jnp.where(seen, lse, HIDDEN)
    arrived(dl, dl_recv.at[1])

    def grads(h, j):
        def one(role, _):
            key = kv[j, h, role, 0]
            value = kv[j, h, role, 1]
            dk = jnp.zeros((KEYS, HD), f32)
            dv = jnp.zeros((KEYS, HD), f32)
            for t in range(GROUP // BQ):
                rows = pl.ds(t * BQ, BQ)
                query = qg[h, role, 0, rows]
                grad = qg[h, role, 1, rows]
                score = dot(key, query, 1, 1)
                prob = jnp.exp2(score * (SCALE * LOG2E) - lse3[role, j, pl.ds(h, 1), rows])
                dprob = dot(value, grad, 1, 1)
                dscore = (prob * (dprob - dl[role, pl.ds(h, 1), rows])).astype(bf16)
                dv += dot(prob.astype(bf16), grad, 1, 0)
                dk += dot(dscore, query, 1, 0)
                step = dot(key, dscore, 0, 0)
                if j == 0:
                    dq[h, role, :, rows] = step
                else:
                    dq[h, role, :, rows] += step
            if j == 0:
                own[h, role, 0] = dk
                own[h, role, 1] = dv
            else:
                part[j - 1, h, role, 0] = dk.astype(bf16)
                part[j - 1, h, role, 1] = dv.astype(bf16)

        one(0, 0)
        one(1, 0)

    def put(which, out, h):
        for role in (0, 1):
            cols = head_cols(SET[role], h)
            remote(
                stage.at[which, h, role, FAR], out.at[:, cols],
                out_send.at[which, h], out_recv.at[which], at_rank(-SIDE[role]),
            )
            pltpu.make_async_copy(stage.at[which, h, role, NEAR], out.at[:, cols], out_recv.at[which]).start()

    def share_dq(h):
        for role in (0, 1):
            stage[0, h, role, NEAR] = dq[h, role, :, block(SIDE[role])].T.astype(bf16)
            stage[0, h, role, FAR] = dq[h, role, :, block(2)].T.astype(bf16)
            remote(stage.at[0, h, role], dq_in.at[h, 1 - role], dq_send.at[h], dq_recv.at[h], at_rank(SIDE[role]))

    def finish_dq(h):
        arrived(dq_in.at[h], dq_recv.at[h])
        arrived(stage.at[0, h], dq_send.at[h])
        for role in (0, 1):
            for where, p in ((NEAR, 0), (FAR, -SIDE[role])):
                total = dq[h, role, :, block(p)].T + dq_in[h, role, where].astype(f32)
                stage[0, h, role, where] = (total * SCALE).astype(bf16)
        put(0, q_out, h)

    def finish_kv(h):
        arrived(back1.at[h], back_recv.at[0, h])

        @pl.when(even)
        def _():
            arrived(back2.at[h], back_recv.at[1, h])
            for n, factor in ((0, SCALE), (1, 1.0)):
                for role in (0, 1):
                    total = own[h, role, n] + back1[h, role, n].astype(f32) + back2[h, role, n].astype(f32)
                    stage[1 + n, h, role] = (total * factor).astype(bf16)

        @pl.when(odd)
        def _():
            for n, factor in ((0, SCALE), (1, 1.0)):
                for role in (0, 1):
                    total = own[h, role, n] + back1[h, role, n].astype(f32)
                    stage[1 + n, h, role] = (total * factor).astype(bf16)

    def put_kv(h):
        put(1, k_out, h)
        put(2, v_out, h)

    def several(first, last, do):
        def each(h, _):
            do(h)
            return 0

        lax.fori_loop(first, last, each, 0)

    def step(i, _):
        @pl.when(i + AHEAD < HEADS)
        def _():
            fetch_outer(i + AHEAD)

        @pl.when(i + AHEAD + 1 < HEADS)
        def _():
            fetch_kv(i + AHEAD + 1)

        @pl.when(i < HEADS)
        def _():
            arrived(qg.at[i, :, :, pl.ds(0, GROUP - ROWS)], q_in_sem.at[i])

        @pl.when(i == HOLD)
        def _():
            several(0, HOLD - 2, put_kv)
            several(EARLY, HOLD, share_dq)

        @pl.when(i < HEADS)
        def _():
            arrived(kv.at[1, i], kv_recv.at[0, i])

            @pl.when(even)
            def _():
                remote(kv.at[1, i], kv.at[2, i], kv_send.at[2, i], kv_recv.at[1, i], at_ctx(1))

            grads(i, 0)

        @pl.when(i + 1 < HEADS)
        def _():
            forward(i + 1)

        @pl.when(i + 2 < HEADS)
        def _():
            give(i + 2)

        @pl.when(i + AHEAD < HEADS)
        def _():
            fetch_own(i + AHEAD)

        inner = i < HEADS

        @pl.when(inner)
        def _():
            h = i
            grads(h, 1)

            @pl.when(odd)
            def _():
                remote(part.at[0, h], back1.at[h], part_send.at[0, h], back_recv.at[0, h], at_ctx(-1))

            arrived(kv.at[2, h], kv_recv.at[1, h])
            grads(h, 2)

            @pl.when(odd)
            def _():
                remote(part.at[1, h], relay.at[h], part_send.at[1, h], relay_recv.at[h], at_ctx(-1))

            @pl.when(even)
            def _():
                remote(part.at[1, h], back2.at[h], part_send.at[1, h], back_recv.at[1, h], at_ctx(-2))

        @pl.when(jnp.logical_and(inner, even))
        def _():
            h = i
            arrived(relay.at[h], relay_recv.at[h])
            for role in (0, 1):
                for n in (0, 1):
                    total = part[0, h, role, n].astype(f32) + relay[h, role, n].astype(f32)
                    part[0, h, role, n] = total.astype(bf16)
            remote(part.at[0, h], back1.at[h], part_send.at[0, h], back_recv.at[0, h], at_ctx(-1))

        @pl.when(jnp.logical_and(i >= 1, i <= EARLY))
        def _():
            share_dq(i - 1)

        @pl.when(i == HOLD)
        def _():
            share_dq(HOLD)

        @pl.when(i >= 2)
        def _():
            finish_kv(i - 2)

        @pl.when(i >= HOLD)
        def _():
            put_kv(i - 2)

        @pl.when(i == HOLD)
        def _():
            several(0, HOLD - 1, finish_dq)

        @pl.when(i > HOLD)
        def _():
            finish_dq(i - 2)

        return 0

    lax.fori_loop(0, HEADS + 2, step, 0)

    arrived(lse_in, dl_send.at[0])
    for r in range(1, RANKS):
        arrived(dl_src.at[pl.ds(0, 2)], dl_send.at[1])

    def drain(h, _):
        arrived(qg.at[h, :, :, pl.ds(0, GROUP - ROWS)], in_send.at[h])
        arrived(qg.at[h, :, :, NEAR], fwd_send.at[h])
        arrived(kv.at[0, h], kv_send.at[0, h])
        arrived(part.at[0, h], part_send.at[0, h])
        arrived(part.at[1, h], part_send.at[1, h])
        for n in range(3):
            arrived(stage.at[n, h, :, NEAR], out_send.at[n, h])

        @pl.when(even)
        def _():
            arrived(kv.at[0, h], kv_send.at[1, h])
            arrived(kv.at[1, h], kv_send.at[2, h])

        return 0

    lax.fori_loop(0, HEADS, drain, 0)
    arrived(q_out, out_recv.at[0])
    arrived(k_out, out_recv.at[1])
    arrived(v_out, out_recv.at[2])


def local(queries, keys, values, outputs, out_grad, logsumexp, clip_of_group):
    hbm = pl.BlockSpec(memory_space=pl.ANY)
    vmem = pl.BlockSpec(memory_space=pltpu.VMEM)
    smem = pl.BlockSpec(memory_space=pltpu.SMEM)
    dma = pltpu.SemaphoreType.DMA
    half = (HEADS, 2, 2, KEYS, HD)
    out = jax.ShapeDtypeStruct((ROWS, RANKS * HEADS * HD), bf16)
    near = pltpu.VMEM((ROWS, RANKS * HEADS * HD), bf16)
    grads = pl.pallas_call(
        kernel,
        out_shape=(near, near, near),
        in_specs=[hbm, hbm, hbm, hbm, hbm, vmem, smem],
        out_specs=(hbm, hbm, hbm),
        scratch_shapes=[
            pltpu.VMEM((HEADS, 2, 2, GROUP, HD), bf16),
            pltpu.VMEM((3, *half), bf16),
            pltpu.VMEM(half, f32),
            pltpu.VMEM((HEADS, 2, HD, GROUP), f32),
            pltpu.VMEM((HEADS, 2, KEYS, HD), bf16),
            pltpu.VMEM((2, *half), bf16),
            pltpu.VMEM(half, bf16),
            pltpu.VMEM(half, bf16),
            pltpu.VMEM(half, bf16),
            pltpu.VMEM((3, HEADS, 2, KEYS, HD), bf16),
            pltpu.VMEM((RANKS, 8, ROWS), f32),
            pltpu.VMEM((2, 8, GROUP), f32),
            pltpu.VMEM((HEADS, GROUP), f32),
            pltpu.VMEM((2, 3, HEADS, GROUP), f32),
            dma((HEADS,)),
            dma((HEADS,)),
            dma((HEADS,)),
            dma((HEADS,)),
            dma((HEADS,)),
            dma((3, HEADS)),
            dma((2, HEADS)),
            dma((2, HEADS)),
            dma((HEADS,)),
            dma((2, HEADS)),
            dma((HEADS,)),
            dma((HEADS,)),
            dma((3, HEADS)),
            dma((3,)),
            dma((2,)),
            dma((2,)),
            dma,
        ],
        cost_estimate=pl.CostEstimate(
            flops=2 * 5 * 3 * HEADS * GROUP * GROUP * HD,
            bytes_accessed=12 * 2**20,
            transcendentals=3 * HEADS * GROUP * GROUP,
        ),
        compiler_params=pltpu.CompilerParams(
            collective_id=0, has_side_effects=True, vmem_limit_bytes=53 * 2**20
        ),
        name="clip_attention_backward",
    )(queries, keys, values, outputs, out_grad, logsumexp, clip_of_group)

    return grads


def solution(mesh):
    rows = P(("ctx", "head"), None)
    return jax.shard_map(
        local,
        mesh=mesh,
        in_specs=(rows, rows, rows, rows, rows, P("head", "ctx"), P()),
        out_specs=(rows, rows, rows),
        check_vma=False,
    )
```

```python
import jax
import jax.numpy as jnp
from jax import lax
from jax.experimental import pallas as pl
from jax.experimental.pallas import tpu as pltpu
from jax.sharding import PartitionSpec as P

HD = 128
GROUP = 1024
HEADS = 6
RANKS = 4
COUNT = 32
ROWS = GROUP // RANKS
KEYS = 2 * ROWS
BQ = 1024
AHEAD = 2
HOLD = 5
EARLY = 4
MESH = pl.DeviceIdType.MESH
SCALE = HD**-0.5
LOG2E = 1.4426950408889634
HIDDEN = 1e30
f32, bf16 = jnp.float32, jnp.bfloat16


def dot(a, b, ca, cb):
    return lax.dot_general(a, b, (((ca,), (cb,)), ((), ())), preferred_element_type=f32)


def kernel(
    q_in, k_in, v_in, o_in, g_in, lse_in, clip_in,
    q_out, k_out, v_out,
    qg, kv, own, dq, dq_in, part, relay, back1, back2, stage, dl_src, dl, lse_far, lse3,
    in_send, kv_in, outer_in, q_in_sem, fwd_send, kv_send, kv_recv, part_send, relay_recv, back_recv,
    dq_send, dq_recv, out_send, out_recv, dl_send, dl_recv, loc,
):
    x = lax.axis_index("head")
    c = lax.axis_index("ctx")
    even = lax.rem(c, 2) == 0
    odd = lax.rem(c, 2) == 1

    def rank(p):
        return lax.rem(x + p + RANKS, RANKS)

    def at_rank(p):
        return {"head": rank(p)}

    def at_ctx(d):
        return {"ctx": lax.rem(c + d + COUNT, COUNT)}

    def arrived(ref, sem):
        pltpu.make_async_copy(ref, ref, sem).wait()

    def remote(src, dst, send, recv, device):
        pltpu.make_async_remote_copy(
            src_ref=src, dst_ref=dst, send_sem=send, recv_sem=recv,
            device_id=device, device_id_type=MESH,
        ).start()

    def block(p):
        return pl.ds(pl.multiple_of(rank(p) * ROWS, ROWS), ROWS)

    def head_cols(p, h):
        return pl.ds(pl.multiple_of((rank(p) * HEADS + h) * HD, HD), HD)

    SIDE = (1, -1)
    SET = (0, -1)
    NEAR, FAR = pl.ds(0, ROWS), pl.ds(ROWS, ROWS)

    barrier = pltpu.get_barrier_semaphore()
    for p in range(1, RANKS):
        pl.semaphore_signal(barrier, inc=1, device_id=at_rank(p), device_id_type=MESH)
    for d in (-2, -1, 1, 2):
        pl.semaphore_signal(barrier, inc=1, device_id=at_ctx(d), device_id_type=MESH)

    def load(h, _):
        for r in range(RANKS):
            cols = pl.ds(pl.multiple_of((r * HEADS + h) * HD, HD), HD)
            pltpu.make_async_copy(o_in.at[:, cols], stage.at[r // 2, h, r % 2, NEAR], loc).start()
            pltpu.make_async_copy(g_in.at[:, cols], stage.at[r // 2, h, r % 2, FAR], loc).start()
        return 0

    lax.fori_loop(0, HEADS, load, 0)
    pl.semaphore_wait(barrier, RANKS - 1 + 4)

    def fetch_outer(h):
        for role in (0, 1):
            side = SIDE[role]
            cols = head_cols(side + SET[role], h)
            for n, src in ((0, q_in), (1, g_in)):
                remote(src.at[:, cols], qg.at[h, role, n, block(0)], in_send.at[h], outer_in.at[h], at_rank(side))

    def fetch_kv(h):
        for role in (0, 1):
            side = SIDE[role]
            cols = head_cols(side + SET[role], h)
            for n, src in ((0, k_in), (1, v_in)):
                remote(src.at[:, cols], kv.at[0, h, role, n, FAR], in_send.at[h], kv_in.at[h], at_rank(side))
        for role in (0, 1):
            cols = head_cols(SET[role], h)
            for n, src in ((0, k_in), (1, v_in)):
                pltpu.make_async_copy(src.at[:, cols], kv.at[0, h, role, n, NEAR], kv_in.at[h]).start()

    def fetch_own(h):
        for role in (0, 1):
            cols = head_cols(SET[role], h)
            for n, src in ((0, q_in), (1, g_in)):
                remote(
                    src.at[:, cols], qg.at[h, 1 - role, n, block(0)],
                    in_send.at[h], q_in_sem.at[h], at_rank(SIDE[role]),
                )
                pltpu.make_async_copy(src.at[:, cols], qg.at[h, role, n, block(0)], q_in_sem.at[h]).start()

    def forward(h):
        arrived(qg.at[h, :, :, NEAR], outer_in.at[h])
        for role in (0, 1):
            outer = block(-SIDE[role])
            remote(
                qg.at[h, role, :, outer], qg.at[h, 1 - role, :, outer],
                fwd_send.at[h], q_in_sem.at[h], at_rank(SIDE[role]),
            )

    def give(h):
        arrived(kv.at[0, h], kv_in.at[h])
        remote(kv.at[0, h], kv.at[1, h], kv_send.at[0, h], kv_recv.at[0, h], at_ctx(1))

        @pl.when(even)
        def _():
            remote(kv.at[0, h], kv.at[2, h], kv_send.at[1, h], kv_recv.at[1, h], at_ctx(2))

    fetch_kv(0)
    fetch_outer(0)
    fetch_own(0)
    fetch_kv(1)
    remote(lse_in, lse_far, dl_send.at[0], dl_recv.at[0], at_rank(1))

    arrived(stage.at[pl.ds(0, 2)], loc)
    lane = lax.broadcasted_iota(jnp.int32, (ROWS, HD), 1)
    delta = jnp.zeros((ROWS, HD), f32)
    for r in range(RANKS):
        for h in range(HEADS):
            prod = stage[r // 2, h, r % 2, NEAR].astype(f32) * stage[r // 2, h, r % 2, FAR].astype(f32)
            total = jnp.sum(prod, axis=1, keepdims=True)
            delta = jnp.where(lane == r * 8 + h, total, delta)
    flipped = delta.T
    for r in range(RANKS):
        dl_src[r] = flipped[r * 8 : (r + 1) * 8]
    for role in (0, 1):
        for p in range(RANKS):
            src, dst = dl_src.at[rank(p + SET[role])], dl.at[role, :, block(0)]
            if p == 0:
                pltpu.make_async_copy(src, dst, dl_recv.at[1]).start()
            else:
                remote(src, dst, dl_send.at[1], dl_recv.at[1], at_rank(p))

    fetch_outer(1)
    forward(0)
    give(0)
    fetch_own(1)
    fetch_kv(2)
    give(1)

    arrived(lse_far, dl_recv.at[0])
    here = clip_in[c]
    for role, src in ((0, lse_in), (1, lse_far)):
        lse = src[...] * LOG2E
        lse3[role, 0] = lse
        for j in (1, 2):
            seen = jnp.logical_and(clip_in[lax.max(c - j, 0)] == here, c >= j)
            lse3[role, j] = jnp.where(seen, lse, HIDDEN)
    arrived(dl, dl_recv.at[1])

    def grads(h, j):
        def one(role, _):
            key = kv[j, h, role, 0]
            value = kv[j, h, role, 1]
            dk = jnp.zeros((KEYS, HD), f32)
            dv = jnp.zeros((KEYS, HD), f32)
            for t in range(GROUP // BQ):
                rows = pl.ds(t * BQ, BQ)
                query = qg[h, role, 0, rows]
                grad = qg[h, role, 1, rows]
                score = dot(key, query, 1, 1)
                prob = jnp.exp2(score * (SCALE * LOG2E) - lse3[role, j, pl.ds(h, 1), rows])
                dprob = dot(value, grad, 1, 1)
                dscore = (prob * (dprob - dl[role, pl.ds(h, 1), rows])).astype(bf16)
                dv += dot(prob.astype(bf16), grad, 1, 0)
                dk += dot(dscore, query, 1, 0)
                step = dot(key, dscore, 0, 0)
                if j == 0:
                    dq[h, role, :, rows] = step
                else:
                    dq[h, role, :, rows] += step
            if j == 0:
                own[h, role, 0] = dk
                own[h, role, 1] = dv
            else:
                part[j - 1, h, role, 0] = dk.astype(bf16)
                part[j - 1, h, role, 1] = dv.astype(bf16)

        one(0, 0)
        one(1, 0)

    def put(which, out, h):
        for role in (0, 1):
            cols = head_cols(SET[role], h)
            remote(
                stage.at[which, h, role, FAR], out.at[:, cols],
                out_send.at[which, h], out_recv.at[which], at_rank(-SIDE[role]),
            )
            pltpu.make_async_copy(stage.at[which, h, role, NEAR], out.at[:, cols], out_recv.at[which]).start()

    def share_dq(h):
        for role in (0, 1):
            stage[0, h, role, NEAR] = dq[h, role, :, block(SIDE[role])].T.astype(bf16)
            stage[0, h, role, FAR] = dq[h, role, :, block(2)].T.astype(bf16)
            remote(stage.at[0, h, role], dq_in.at[h, 1 - role], dq_send.at[h], dq_recv.at[h], at_rank(SIDE[role]))

    def finish_dq(h):
        arrived(dq_in.at[h], dq_recv.at[h])
        arrived(stage.at[0, h], dq_send.at[h])
        for role in (0, 1):
            for where, p in ((NEAR, 0), (FAR, -SIDE[role])):
                total = dq[h, role, :, block(p)].T + dq_in[h, role, where].astype(f32)
                stage[0, h, role, where] = (total * SCALE).astype(bf16)
        put(0, q_out, h)

    def finish_kv(h):
        arrived(back1.at[h], back_recv.at[0, h])

        @pl.when(even)
        def _():
            arrived(back2.at[h], back_recv.at[1, h])
            for n, factor in ((0, SCALE), (1, 1.0)):
                for role in (0, 1):
                    total = own[h, role, n] + back1[h, role, n].astype(f32) + back2[h, role, n].astype(f32)
                    stage[1 + n, h, role] = (total * factor).astype(bf16)

        @pl.when(odd)
        def _():
            for n, factor in ((0, SCALE), (1, 1.0)):
                for role in (0, 1):
                    total = own[h, role, n] + back1[h, role, n].astype(f32)
                    stage[1 + n, h, role] = (total * factor).astype(bf16)

    def put_kv(h):
        put(1, k_out, h)
        put(2, v_out, h)

    def several(first, last, do):
        def each(h, _):
            do(h)
            return 0

        lax.fori_loop(first, last, each, 0)

    def step(i, _):
        @pl.when(i + AHEAD < HEADS)
        def _():
            fetch_outer(i + AHEAD)

        @pl.when(i + AHEAD + 1 < HEADS)
        def _():
            fetch_kv(i + AHEAD + 1)

        @pl.when(i < HEADS)
        def _():
            arrived(qg.at[i, :, :, pl.ds(0, GROUP - ROWS)], q_in_sem.at[i])

        @pl.when(i == HOLD)
        def _():
            several(0, HOLD - 2, put_kv)
            several(EARLY, HOLD, share_dq)

        @pl.when(i < HEADS)
        def _():
            arrived(kv.at[1, i], kv_recv.at[0, i])

            @pl.when(even)
            def _():
                remote(kv.at[1, i], kv.at[2, i], kv_send.at[2, i], kv_recv.at[1, i], at_ctx(1))

            grads(i, 0)

        @pl.when(i + 1 < HEADS)
        def _():
            forward(i + 1)

        @pl.when(i + 2 < HEADS)
        def _():
            give(i + 2)

        @pl.when(i + AHEAD < HEADS)
        def _():
            fetch_own(i + AHEAD)

        inner = i < HEADS

        @pl.when(inner)
        def _():
            h = i
            grads(h, 1)

            @pl.when(odd)
            def _():
                remote(part.at[0, h], back1.at[h], part_send.at[0, h], back_recv.at[0, h], at_ctx(-1))

            arrived(kv.at[2, h], kv_recv.at[1, h])
            grads(h, 2)

            @pl.when(odd)
            def _():
                remote(part.at[1, h], relay.at[h], part_send.at[1, h], relay_recv.at[h], at_ctx(-1))

            @pl.when(even)
            def _():
                remote(part.at[1, h], back2.at[h], part_send.at[1, h], back_recv.at[1, h], at_ctx(-2))

        @pl.when(jnp.logical_and(inner, even))
        def _():
            h = i
            arrived(relay.at[h], relay_recv.at[h])
            for role in (0, 1):
                for n in (0, 1):
                    total = part[0, h, role, n].astype(f32) + relay[h, role, n].astype(f32)
                    part[0, h, role, n] = total.astype(bf16)
            remote(part.at[0, h], back1.at[h], part_send.at[0, h], back_recv.at[0, h], at_ctx(-1))

        @pl.when(jnp.logical_and(i >= 1, i <= EARLY))
        def _():
            share_dq(i - 1)

        @pl.when(jnp.logical_and(i >= HOLD, i < HEADS))
        def _():
            share_dq(i)

        @pl.when(i >= 2)
        def _():
            finish_kv(i - 2)

        @pl.when(i >= HOLD)
        def _():
            put_kv(i - 2)

        @pl.when(i == HOLD)
        def _():
            several(0, HOLD - 1, finish_dq)

        @pl.when(i > HOLD)
        def _():
            finish_dq(i - 2)

        return 0

    lax.fori_loop(0, HEADS + 2, step, 0)

    arrived(lse_in, dl_send.at[0])
    for r in range(1, RANKS):
        arrived(dl_src.at[pl.ds(0, 2)], dl_send.at[1])

    def drain(h, _):
        arrived(qg.at[h, :, :, pl.ds(0, GROUP - ROWS)], in_send.at[h])
        arrived(qg.at[h, :, :, NEAR], fwd_send.at[h])
        arrived(kv.at[0, h], kv_send.at[0, h])
        arrived(part.at[0, h], part_send.at[0, h])
        arrived(part.at[1, h], part_send.at[1, h])
        for n in range(3):
            arrived(stage.at[n, h, :, NEAR], out_send.at[n, h])

        @pl.when(even)
        def _():
            arrived(kv.at[0, h], kv_send.at[1, h])
            arrived(kv.at[1, h], kv_send.at[2, h])

        return 0

    lax.fori_loop(0, HEADS, drain, 0)
    arrived(q_out, out_recv.at[0])
    arrived(k_out, out_recv.at[1])
    arrived(v_out, out_recv.at[2])


def local(queries, keys, values, outputs, out_grad, logsumexp, clip_of_group):
    hbm = pl.BlockSpec(memory_space=pl.ANY)
    vmem = pl.BlockSpec(memory_space=pltpu.VMEM)
    smem = pl.BlockSpec(memory_space=pltpu.SMEM)
    dma = pltpu.SemaphoreType.DMA
    half = (HEADS, 2, 2, KEYS, HD)
    out = jax.ShapeDtypeStruct((ROWS, RANKS * HEADS * HD), bf16)
    near = pltpu.VMEM((ROWS, RANKS * HEADS * HD), bf16)
    grads = pl.pallas_call(
        kernel,
        out_shape=(near, near, near),
        in_specs=[hbm, hbm, hbm, hbm, hbm, vmem, smem],
        out_specs=(hbm, hbm, hbm),
        scratch_shapes=[
            pltpu.VMEM((HEADS, 2, 2, GROUP, HD), bf16),
            pltpu.VMEM((3, *half), bf16),
            pltpu.VMEM(half, f32),
            pltpu.VMEM((HEADS, 2, HD, GROUP), f32),
            pltpu.VMEM((HEADS, 2, KEYS, HD), bf16),
            pltpu.VMEM((2, *half), bf16),
            pltpu.VMEM(half, bf16),
            pltpu.VMEM(half, bf16),
            pltpu.VMEM(half, bf16),
            pltpu.VMEM((3, HEADS, 2, KEYS, HD), bf16),
            pltpu.VMEM((RANKS, 8, ROWS), f32),
            pltpu.VMEM((2, 8, GROUP), f32),
            pltpu.VMEM((HEADS, GROUP), f32),
            pltpu.VMEM((2, 3, HEADS, GROUP), f32),
            dma((HEADS,)),
            dma((HEADS,)),
            dma((HEADS,)),
            dma((HEADS,)),
            dma((HEADS,)),
            dma((3, HEADS)),
            dma((2, HEADS)),
            dma((2, HEADS)),
            dma((HEADS,)),
            dma((2, HEADS)),
            dma((HEADS,)),
            dma((HEADS,)),
            dma((3, HEADS)),
            dma((3,)),
            dma((2,)),
            dma((2,)),
            dma,
        ],
        cost_estimate=pl.CostEstimate(
            flops=2 * 5 * 3 * HEADS * GROUP * GROUP * HD,
            bytes_accessed=12 * 2**20,
            transcendentals=3 * HEADS * GROUP * GROUP,
        ),
        compiler_params=pltpu.CompilerParams(
            collective_id=0, has_side_effects=True, vmem_limit_bytes=53 * 2**20
        ),
        name="clip_attention_backward",
    )(queries, keys, values, outputs, out_grad, logsumexp, clip_of_group)

    def write(*refs):
        copies = [pltpu.make_async_copy(refs[n], refs[3 + n], refs[6].at[n]) for n in range(3)]
        for copy in copies:
            copy.start()
        for copy in copies:
            copy.wait()

    return pl.pallas_call(
        write,
        out_shape=(out,) * 3,
        in_specs=[hbm] * 3,
        out_specs=(hbm,) * 3,
        scratch_shapes=[dma((3,))],
        compiler_params=pltpu.CompilerParams(vmem_limit_bytes=4 * 2**20),
        name="write_out",
    )(*(pltpu.with_memory_space_constraint(grad, pltpu.VMEM) for grad in grads))


def solution(mesh):
    rows = P(("ctx", "head"), None)
    return jax.shard_map(
        local,
        mesh=mesh,
        in_specs=(rows, rows, rows, rows, rows, P("head", "ctx"), P()),
        out_specs=(rows, rows, rows),
        check_vma=False,
    )
```
